32 devices in a mesh: dp: 32 (over z, y, x, core).
Axes of the slice: x: 2, y: 2, z: 4, core: 2. Of those that a mesh axis runs over, the one named last changes fastest.
Arguments:
- tokens: bfloat16 [4096, 1024], P('dp'), may hold values from -6 to 6
- segment_ids: int32 [4096], P('dp'), may hold values from 0 to 2, as said below
- pad_mask: int32 [4096], P('dp'), may hold values from 0 to 1, as said below
- ln1_gain: bfloat16 [1024], P('dp'), may hold values from 0.5 to 1.5
- ln1_bias: bfloat16 [1024], P('dp'), may hold values from -1.796875 to 1.796875
- qkv_weight: bfloat16 [1024, 3072], P('dp'), may hold values from -0.1875 to 0.1875
- qkv_bias: bfloat16 [2048], P('dp'), may hold values from -1.796875 to 1.796875
- out_weight: bfloat16 [1024, 1024], P('dp'), may hold values from -1 to 1
- out_bias: bfloat16 [1024], P('dp'), may hold values from -1.796875 to 1.796875
- ln2_gain: bfloat16 [1024], P('dp'), may hold values from 0.5 to 1.5
- ln2_bias: bfloat16 [1024], P('dp'), may hold values from -1.796875 to 1.796875
- up_weight: bfloat16 [1024, 4096], P('dp'), may hold values from -0.1875 to 0.1875
- up_bias: bfloat16 [4096], P('dp'), may hold values from -1.796875 to 1.796875
- down_weight: bfloat16 [4096, 1024], P('dp'), may hold values from -0.09375 to 0.09375
- down_bias: bfloat16 [1024], P('dp'), may hold values from -1.796875 to 1.796875
- cotangent: bfloat16 [4096, 1024], P('dp'), may hold values from -6 to 6
Outputs:
- block_out: bfloat16 [4096, 1024], P('dp')
- grad_tokens: float32 [4096, 1024], P('dp')
- grad_ln1_gain: float32 [1024], P('dp')
- grad_ln1_bias: float32 [1024], P('dp')
- grad_qkv_weight: float32 [1024, 3072], P('dp')
- grad_qkv_bias: float32 [2048], P('dp')
- grad_out_weight: float32 [1024, 1024], P('dp')
- grad_out_bias: float32 [1024], P('dp')
- grad_ln2_gain: float32 [1024], P('dp')
- grad_ln2_bias: float32 [1024], P('dp')
- grad_up_weight: float32 [1024, 4096], P('dp')
- grad_up_bias: float32 [4096], P('dp')
- grad_down_weight: float32 [4096, 1024], P('dp')
- grad_down_bias: float32 [1024], P('dp')
The draws below stay inside these ranges and needn't reach their ends.
Inputs may be any that keep to these rules, and one draw needn't show every extreme that they name: `segment_ids`: along one device's 128 slots the numbers never fall; padding slots carry the number of the device's last sequence. `pad_mask`: on each device the live slots come first, 64 or more of them; some device has all 128 slots live.
All inputs are finite; a program needn't handle non-finite values.
Results may differ from the reference program's by a relative error of at most 0.0092.
Values may be sent and summed in bfloat16 or wider, within the bound.
No kernel may reach another device: no remote copies, remote signals or barrier semaphores. Data moves between devices by JAX's collectives and lax.ppermute only.
A program may use at most 256 MiB of HBM per device.

```python
import math
import jax
import jax.numpy as jnp
from jax import lax

D = 1024
FF = 4096
HEADS = 16
HEAD_DIM = 64
TOK_DEV = 128
TOKENS = 4096
N_DP = 32


def slot_layout(key):
    key_short, key_full, key_cut, key_used = jax.random.split(key, 4)
    shortfall = jax.random.randint(key_short, (N_DP,), 0, TOK_DEV // 2 + 1)
    full_device = jax.random.randint(key_full, (), 0, N_DP)
    devices = jnp.arange(N_DP, dtype=jnp.int32)
    live_count = jnp.where(devices == full_device, TOK_DEV, TOK_DEV - shortfall)
    cut_raw = jax.random.randint(key_cut, (N_DP, 2), 0, 1 << 20)
    cut_points = 1 + cut_raw % (live_count[:, None] - 1)
    used = jax.random.randint(key_used, (N_DP, 2), 0, 2)
    used = jnp.where((devices == full_device)[:, None], 0, used)
    cut_points = jnp.where(used == 1, cut_points, TOK_DEV)
    positions = jnp.arange(TOK_DEV, dtype=jnp.int32)
    segments = jnp.sum((positions[None, :, None] >= cut_points[:, None, :]).astype(jnp.int32), axis=-1)
    live = (positions[None, :] < live_count[:, None]).astype(jnp.int32)
    return (segments.reshape(N_DP * TOK_DEV), live.reshape(N_DP * TOK_DEV))


def draw_segment_ids(key, part):
    shared = slot_layout(key)
    return shared[0]


def draw_pad_mask(key, part):
    shared = slot_layout(key)
    return shared[1]


def shard_levels(own_key, extent, cuts, smallest, top_value):
    level = 1.0
    for dim, parts in cuts:
        steps = jax.random.uniform(jax.random.fold_in(jax.random.fold_in(own_key, 6), dim), (parts,), jnp.float32, smallest / len(cuts), top_value / len(cuts))
        level = level * jnp.repeat(jnp.exp(steps), extent[dim] // parts).reshape((-1,) + (1,) * (len(extent) - 1 - dim))
    return level


def scatter_about(stream_key, shape, scale, reach, shards=(), kind=jnp.bfloat16):
    result = scale * jax.random.normal(stream_key, shape, jnp.float32)
    if shards:
        result = result * shard_levels(stream_key, shape, shards, -0.22, 0.18)
    return jnp.clip(result, -reach, reach).astype(kind)


def setup_inputs(seed: int = 0) -> dict:
    arg_keys = jax.random.split(jax.random.key(seed), 17)
    return {
        "tokens": scatter_about(arg_keys[0], (TOKENS, D), 1.0, 6.0, ((0, 32),)),
        "segment_ids": draw_segment_ids(jax.random.fold_in(arg_keys[16], 71), 0),
        "pad_mask": draw_pad_mask(jax.random.fold_in(arg_keys[16], 71), 0),
        "ln1_gain": jnp.clip(1.0 + 0.1 * jax.random.normal(arg_keys[3], (D,), jnp.float32), 0.5, 1.5).astype(jnp.bfloat16),
        "ln1_bias": scatter_about(arg_keys[4], (D,), 0.3, 1.796875, ((0, 32),)),
        "qkv_weight": scatter_about(arg_keys[5], (D, 3 * D), D ** -0.5, 0.1875, ((0, 32),)),
        "qkv_bias": scatter_about(arg_keys[6], (2 * D,), 0.3, 1.796875, ((0, 32),)),
        "out_weight": scatter_about(arg_keys[7], (D, D), (D // 32) ** -0.5, 1.0, ((0, 32),)),
        "out_bias": scatter_about(arg_keys[8], (D,), 0.3, 1.796875, ((0, 32),)),
        "ln2_gain": jnp.clip(1.0 + 0.1 * jax.random.normal(arg_keys[9], (D,), jnp.float32), 0.5, 1.5).astype(jnp.bfloat16),
        "ln2_bias": scatter_about(arg_keys[10], (D,), 0.3, 1.796875, ((0, 32),)),
        "up_weight": scatter_about(arg_keys[11], (D, FF), D ** -0.5, 0.1875, ((0, 32),)),
        "up_bias": scatter_about(arg_keys[12], (FF,), 0.3, 1.796875, ((0, 32),)),
        "down_weight": scatter_about(arg_keys[13], (FF, D), FF ** -0.5, 0.09375, ((0, 32),)),
        "down_bias": scatter_about(arg_keys[14], (D,), 0.3, 1.796875, ((0, 32),)),
        "cotangent": scatter_about(arg_keys[15], (TOKENS, D), 1.0, 6.0, ((0, 32),)),
    }


EPS = 1e-05
NEG = -1e+30
HIGH = lax.Precision.HIGHEST

@jax.custom_vjp
def low(v):
    return lax.optimization_barrier(v.astype(jnp.bfloat16)).astype(jnp.float32)

@jax.custom_vjp
def low_back(v):
    return v

def low_keep(v):
    return (low(v), None)

def low_pass(kept, grad):
    return (grad,)

def back_keep(v):
    return (v, None)

def back_low(kept, grad):
    return (low(grad),)
low.defvjp(low_keep, low_pass)
low_back.defvjp(back_keep, back_low)

def layer_norm(inputs, gain, offset):
    average = lax.optimization_barrier(jnp.mean(inputs, axis=-1, keepdims=True))
    centered = inputs - average
    variance = lax.optimization_barrier(jnp.mean(centered * centered, axis=-1, keepdims=True))
    return centered * lax.rsqrt(variance + EPS) * gain + offset

def gelu_tanh(inputs):
    return 0.5 * inputs * (1.0 + jnp.tanh(0.7978845608028654 * (inputs + 0.044715 * inputs * inputs * inputs)))

def forward(params, token_rows, allowed):
    gain_one, offset_one, proj_in, proj_bias, proj_out, out_offset, gain_two, offset_two, up_matrix, up_offset, down_matrix, down_offset = params
    row_count = token_rows.shape[0]
    model_width = token_rows.shape[1]
    hidden_one = low(layer_norm(token_rows, gain_one, offset_one))
    bias_full = jnp.concatenate([proj_bias[:model_width], jnp.zeros((model_width,), jnp.float32), proj_bias[model_width:]])
    packed = low_back(low(jnp.dot(hidden_one, proj_in, precision=HIGH) + bias_full))
    queries = packed[:, :model_width].reshape(row_count, HEADS, HEAD_DIM)
    key_rows = packed[:, model_width:2 * model_width].reshape(row_count, HEADS, HEAD_DIM)
    value_rows = packed[:, 2 * model_width:].reshape(row_count, HEADS, HEAD_DIM)
    scores = low_back(jnp.einsum('qhd,khd->hqk', queries, key_rows, precision=HIGH) * (1.0 / math.sqrt(HEAD_DIM)))
    scores = jnp.where(allowed[None], scores, NEG)
    row_max = lax.optimization_barrier(jnp.max(scores, axis=-1, keepdims=True))
    weights_raw = jnp.exp(scores - row_max)
    attention = low(weights_raw / lax.optimization_barrier(jnp.sum(weights_raw, axis=-1, keepdims=True)))
    mixed = jnp.einsum('hqk,khd->qhd', attention, value_rows, precision=HIGH).reshape(row_count, model_width)
    mixed = low_back(low(mixed))
    branch = low_back(jnp.dot(mixed, proj_out, precision=HIGH) + out_offset)
    middle = token_rows + branch
    hidden_two = low(layer_norm(middle, gain_two, offset_two))
    pre_act = low_back(jnp.dot(hidden_two, up_matrix, precision=HIGH) + up_offset)
    activated = low(gelu_tanh(pre_act))
    feed = low_back(jnp.dot(activated, down_matrix, precision=HIGH) + down_offset)
    return middle + feed

def reference(tokens, segment_ids, pad_mask, ln1_gain, ln1_bias, qkv_weight, qkv_bias, out_weight, out_bias, ln2_gain, ln2_bias, up_weight, up_bias, down_weight, down_bias, cotangent):
    params = tuple((weight.astype(jnp.float32) for weight in (ln1_gain, ln1_bias, qkv_weight, qkv_bias, out_weight, out_bias, ln2_gain, ln2_bias, up_weight, up_bias, down_weight, down_bias)))
    model_width = tokens.shape[1]
    token_blocks = tokens.astype(jnp.float32).reshape(N_DP, TOK_DEV, model_width)
    grad_blocks = cotangent.astype(jnp.float32).reshape(N_DP, TOK_DEV, model_width)
    segment_blocks = segment_ids.reshape(N_DP, TOK_DEV)
    mask_blocks = pad_mask.reshape(N_DP, TOK_DEV)
    positions = jnp.arange(TOK_DEV, dtype=jnp.int32)
    causal = positions[None, :] <= positions[:, None]

    def one_device(totals, pieces):
        token_rows, segments, live_mask, grad_rows = pieces
        allowed = (segments[:, None] == segments[None, :]) & causal & (live_mask[None, :] == 1)

        def block_forward(weights, inputs):
            return forward(weights, inputs, allowed)
        outputs, pullback = jax.vjp(block_forward, params, token_rows)
        grad_weights, grad_inputs = pullback(grad_rows * live_mask[:, None].astype(jnp.float32))
        totals = jax.tree.map(jnp.add, totals, grad_weights)
        return (totals, (outputs.astype(jnp.bfloat16), grad_inputs))
    zero_grads = tuple((jnp.zeros(weight.shape, jnp.float32) for weight in params))
    totals, (outputs, grad_inputs) = lax.scan(one_device, zero_grads, (token_blocks, segment_blocks, mask_blocks, grad_blocks))
    return (outputs.reshape(N_DP * TOK_DEV, model_width), grad_inputs.reshape(N_DP * TOK_DEV, model_width), totals[0], totals[1], totals[2], totals[3], totals[4], totals[5], totals[6], totals[7], totals[8], totals[9], totals[10], totals[11])
```

```python
import functools
import math

import jax
import jax.numpy as jnp
from jax import lax
from jax.experimental import pallas as pl
from jax.experimental.pallas import tpu as pltpu
from jax.sharding import PartitionSpec as P

HEAD_DIM = 64
EPS = 1e-05
NEG = -1e30
GROUP = 8
DIRECT_PLANES = 8
LOW = jnp.bfloat16
WIDE = jnp.float32


def norm_rows(inputs):
    average = jnp.mean(inputs, axis=-1, keepdims=True)
    centered = inputs - average
    variance = jnp.mean(centered * centered, axis=-1, keepdims=True)
    inverse = lax.rsqrt(variance + EPS)
    return (centered * inverse, inverse)


def norm_back(grad_in, normed, inverse, gain):
    scaled = grad_in * gain
    return inverse * (
        scaled
        - jnp.mean(scaled, axis=1, keepdims=True)
        - normed * jnp.mean(scaled * normed, axis=1, keepdims=True)
    )


def gelu_tanh(inputs):
    return (
        0.5
        * inputs
        * (1.0 + jnp.tanh(0.7978845608028654 * (inputs + 0.044715 * inputs * inputs * inputs)))
    )


def dot(first, second, dims):
    return lax.dot_general(first, second, (dims, ((), ())), preferred_element_type=jnp.float32)


def plain_dot(first, second):
    return dot(first, second, ((1,), (0,)))


def left_dot(first, second):
    return dot(first, second, ((0,), (0,)))


def right_dot(first, second):
    return dot(first, second, ((1,), (1,)))


def head_masks():
    lane = lax.broadcasted_iota(jnp.int32, (1, 2 * HEAD_DIM), 1)
    return [((lane // HEAD_DIM) == h).astype(LOW) for h in range(2)]


def softmax_rows(query, key, allowed):
    scores = right_dot(query, key) * (1.0 / math.sqrt(HEAD_DIM))
    scores = jnp.where(allowed, scores, NEG)
    top = jnp.max(scores, axis=1, keepdims=True)
    raw = jnp.exp(scores - top)
    return raw / jnp.sum(raw, axis=1, keepdims=True)


def attention_kernel(packed_ref, allowed_ref, out_ref):
    masks = head_masks()
    rows = allowed_ref.shape[1]
    width = 2 * HEAD_DIM
    for block in range(allowed_ref.shape[0]):
        part = pl.ds(block * rows, rows)
        query = packed_ref[part, :width]
        key = packed_ref[part, width : 2 * width]
        value = packed_ref[part, 2 * width :]
        allowed = allowed_ref[block] > 0
        total = None
        for mask in masks:
            weights = softmax_rows(query * mask, key, allowed).astype(LOW)
            term = plain_dot(weights, value * mask)
            total = term if total is None else total + term
        out_ref[part, :] = total.astype(LOW)


def attention_back_kernel(packed_ref, grad_ref, allowed_ref, out_ref):
    masks = head_masks()
    rows = allowed_ref.shape[1]
    width = 2 * HEAD_DIM
    scale = 1.0 / math.sqrt(HEAD_DIM)
    for block in range(allowed_ref.shape[0]):
        part = pl.ds(block * rows, rows)
        query = packed_ref[part, :width]
        key = packed_ref[part, width : 2 * width]
        value = packed_ref[part, 2 * width :]
        grad = grad_ref[part, :]
        allowed = allowed_ref[block] > 0
        sums = [None, None, None]
        for mask in masks:
            query_head = query * mask
            grad_head = grad * mask
            weights = softmax_rows(query_head, key, allowed)
            grad_weights = right_dot(grad_head, value)
            grad_scores = weights * (
                grad_weights - jnp.sum(grad_weights * weights, axis=1, keepdims=True)
            )
            grad_scores = grad_scores.astype(LOW)
            terms = (
                plain_dot(grad_scores, key * mask),
                left_dot(grad_scores, query_head),
                left_dot(weights.astype(LOW), grad_head),
            )
            sums = [t if s is None else s + t for s, t in zip(sums, terms)]
        out_ref[part, :width] = (sums[0] * scale).astype(LOW)
        out_ref[part, width : 2 * width] = (sums[1] * scale).astype(LOW)
        out_ref[part, 2 * width :] = sums[2].astype(LOW)


BLOCKS_STEP = 2


def attention(packed, allowed):
    blocks, rows, _ = allowed.shape
    width = 2 * HEAD_DIM
    step = BLOCKS_STEP
    return pl.pallas_call(
        attention_kernel,
        grid=(blocks // step,),
        in_specs=[
            pl.BlockSpec((step * rows, 3 * width), lambda i: (i, 0)),
            pl.BlockSpec((step, rows, rows), lambda i: (i, 0, 0)),
        ],
        out_specs=pl.BlockSpec((step * rows, width), lambda i: (i, 0)),
        out_shape=jax.ShapeDtypeStruct((blocks * rows, width), LOW),
        cost_estimate=pl.CostEstimate(
            flops=8 * blocks * rows * rows * width,
            bytes_accessed=2 * packed.size + 4 * allowed.size,
            transcendentals=2 * allowed.size,
        ),
    )(packed, allowed)


def attention_back(packed, grad, allowed):
    blocks, rows, _ = allowed.shape
    width = 2 * HEAD_DIM
    step = BLOCKS_STEP
    return pl.pallas_call(
        attention_back_kernel,
        grid=(blocks // step,),
        in_specs=[
            pl.BlockSpec((step * rows, 3 * width), lambda i: (i, 0)),
            pl.BlockSpec((step * rows, width), lambda i: (i, 0)),
            pl.BlockSpec((step, rows, rows), lambda i: (i, 0, 0)),
        ],
        out_specs=pl.BlockSpec((step * rows, 3 * width), lambda i: (i, 0)),
        out_shape=jax.ShapeDtypeStruct((blocks * rows, 3 * width), LOW),
        cost_estimate=pl.CostEstimate(
            flops=20 * blocks * rows * rows * width,
            bytes_accessed=4 * packed.size + 4 * allowed.size,
            transcendentals=2 * allowed.size,
        ),
    )(packed, grad, allowed)


class Links:
    def __init__(self, count):
        self.count = count
        self.planes = count // GROUP
        index = lax.axis_index("dp")
        self.place = index % GROUP
        self.plane = index // GROUP

    def swap(self, array, flip):
        return lax.ppermute(array, "dp", [(i, i ^ flip) for i in range(self.count)])

    def shift(self, array, steps):
        hop = steps * GROUP
        return lax.ppermute(array, "dp", [(i, (i + hop) % self.count) for i in range(self.count)])

    def group_gather(self, block):
        found = {0: block}
        for flip in (6, 2, 4):
            found[flip] = self.swap(block, flip)
        for flip in (0, 2, 4, 6):
            found[flip + 1] = self.swap(found[flip], 1)
        return [found[r] for r in range(GROUP)]

    def group_sum(self, parts):
        half = {}
        for flip in (6, 2, 4, 0):
            half[flip] = parts[flip].astype(WIDE) + self.swap(parts[flip ^ 1].astype(LOW), 1)
        total = half[0]
        for flip in (6, 2, 4):
            total = total + self.swap(half[flip].astype(LOW), flip).astype(WIDE)
        return total

    def exchange(self, parts):
        return [parts[0]] + [self.swap(parts[r], r) for r in range(1, GROUP)]

    def plane_groups(self):
        return [[p * GROUP + j for p in range(self.planes)] for j in range(GROUP)]

    def plane_gather(self, block):
        if self.planes > DIRECT_PLANES:
            return lax.all_gather(block, "dp", axis_index_groups=self.plane_groups())
        found = jnp.zeros((self.planes,) + block.shape, block.dtype)
        found = lax.dynamic_update_index_in_dim(found, block, self.plane, 0)
        for k in range(1, self.planes):
            source = (self.plane + self.planes - k) % self.planes
            found = lax.dynamic_update_index_in_dim(found, self.shift(block, k), source, 0)
        return found

    def plane_sum(self, chunks):
        if self.planes > DIRECT_PLANES:
            return lax.psum_scatter(
                chunks.astype(WIDE), "dp", axis_index_groups=self.plane_groups()
            )
        total = lax.dynamic_index_in_dim(chunks, self.plane, 0, False).astype(WIDE)
        for k in range(1, self.planes):
            target = (self.plane + k) % self.planes
            term = lax.dynamic_index_in_dim(chunks, target, 0, False)
            total = total + self.shift(term, k).astype(WIDE)
        return total


def local(
    tokens,
    segment_ids,
    pad_mask,
    ln1_gain,
    ln1_bias,
    qkv_weight,
    qkv_bias,
    out_weight,
    out_bias,
    ln2_gain,
    ln2_bias,
    up_weight,
    up_bias,
    down_weight,
    down_bias,
    cotangent,
):
    count = lax.axis_size("dp")
    links = Links(count)
    place, planes = links.place, links.planes
    rows, width = tokens.shape
    own_rows = qkv_weight.shape[0]
    hidden = up_weight.shape[1]
    shard = width // GROUP
    hidden_shard = hidden // GROUP
    own_hidden = hidden // count
    heads_width = 3 * shard

    small = jnp.concatenate(
        [ln1_gain, ln1_bias, out_bias, ln2_gain, ln2_bias, down_bias, qkv_bias, up_bias]
    )
    small_size = small.shape[0]
    small_row = jnp.pad(small, (0, heads_width - small_size))[None]
    small_rows = jnp.pad(small_row, ((0, 7), (0, 0)))
    qkv_parts = qkv_weight.reshape(own_rows, 3, GROUP, shard).transpose(2, 0, 1, 3)
    qkv_parts = qkv_parts.reshape(GROUP, own_rows, heads_width)
    sent = []
    for r in range(GROUP):
        piece = lax.dynamic_index_in_dim(qkv_parts, place ^ r, 0, False)
        sent.append(jnp.concatenate([piece, small_rows], axis=0))
    buffer = jnp.zeros((GROUP, own_rows + 8, heads_width), LOW)
    for r, piece in enumerate(links.exchange(sent)):
        buffer = lax.dynamic_update_index_in_dim(buffer, piece, place ^ r, 0)
    buffer = links.plane_gather(buffer)
    qkv_full = buffer[:, :, :own_rows].reshape(width, heads_width)
    small_all = buffer[:, :, own_rows, :small_size].reshape(count, small_size).astype(WIDE)
    gain_one, bias_one, bias_out, gain_two, bias_two, bias_down = (
        small_all[:, i * own_rows : (i + 1) * own_rows].reshape(width) for i in range(6)
    )
    qkv_bias_all = small_all[:, 6 * own_rows : 8 * own_rows].reshape(2, width)
    bias_qv = lax.dynamic_slice_in_dim(qkv_bias_all, place * shard, shard, 1)
    bias_heads = jnp.concatenate([bias_qv[0], jnp.zeros((shard,), WIDE), bias_qv[1]])
    up_bias_all = small_all[:, 8 * own_rows :].reshape(planes, GROUP, own_hidden)
    bias_up = lax.dynamic_index_in_dim(up_bias_all, place, 1, False).reshape(hidden_shard)

    code = (segment_ids * 2 + pad_mask).astype(LOW)
    code_row = jnp.pad(code[None], ((0, 7), (0, width - rows)))
    token_blocks = links.group_gather(jnp.concatenate([tokens, code_row], axis=0))
    token_all = jnp.concatenate([b[:rows] for b in token_blocks], axis=0)
    codes = jnp.stack([b[rows, :rows] for b in token_blocks]).astype(jnp.int32)
    segments, live = codes >> 1, codes & 1
    positions = jnp.arange(rows, dtype=jnp.int32)
    allowed = (
        (segments[:, :, None] == segments[:, None, :])
        & (positions[None, :] <= positions[:, None])[None]
        & (live[:, None, :] == 1)
    ).astype(WIDE)

    up_parts = up_weight.reshape(own_rows, planes, GROUP, own_hidden).transpose(2, 0, 1, 3)
    up_parts = up_parts.reshape(GROUP, own_rows, hidden_shard)
    sent = [lax.dynamic_index_in_dim(up_parts, place ^ r, 0, False) for r in range(GROUP)]
    buffer = jnp.zeros((GROUP, own_rows, hidden_shard), LOW)
    for r, piece in enumerate(links.exchange(sent)):
        buffer = lax.dynamic_update_index_in_dim(buffer, piece, place ^ r, 0)
    out_plane = links.plane_gather(out_weight)
    up_full = links.plane_gather(buffer).reshape(width, hidden_shard)
    down_full = links.plane_gather(down_weight).reshape(hidden_shard, width)
    out_full = jnp.zeros((planes, GROUP, own_rows, width), LOW)
    for r, piece in enumerate(links.group_gather(out_plane)):
        out_full = lax.dynamic_update_index_in_dim(out_full, piece, place ^ r, 1)
    out_full = out_full.reshape(width, width)

    grad_out = cotangent.astype(WIDE) * pad_mask.astype(WIDE)[:, None]
    grad_feed_own = grad_out.astype(LOW)
    grad_feed = jnp.concatenate(links.group_gather(grad_feed_own), axis=0)

    normed_all, _ = norm_rows(token_all.astype(WIDE))
    hidden_one = (normed_all * gain_one + bias_one).astype(LOW)
    packed = (plain_dot(hidden_one, qkv_full) + bias_heads).astype(LOW)
    mixed_heads = attention(packed, allowed).reshape(GROUP, rows, shard)
    mixed = jnp.zeros((rows, width), LOW)
    for r, piece in enumerate(links.exchange([mixed_heads[r] for r in range(GROUP)])):
        mixed = lax.dynamic_update_slice_in_dim(mixed, piece, (place ^ r) * shard, 1)
    token_rows = tokens.astype(WIDE)
    middle = token_rows + (plain_dot(mixed, out_full) + bias_out)
    normed_two, inverse_two = norm_rows(middle)
    hidden_two_own = (normed_two * gain_two + bias_two).astype(LOW)
    hidden_two = jnp.concatenate(links.group_gather(hidden_two_own), axis=0)
    pre_act = plain_dot(hidden_two, up_full) + bias_up
    activated, gelu_pull = jax.vjp(gelu_tanh, pre_act)
    activated_low = activated.astype(LOW)

    (grad_pre,) = gelu_pull(right_dot(grad_feed, down_full))
    grad_pre_low = grad_pre.astype(LOW)
    grad_hidden_parts = right_dot(grad_pre_low, up_full).astype(LOW).reshape(GROUP, rows, width)
    grad_hidden_two = links.group_sum([grad_hidden_parts[r] for r in range(GROUP)])
    feed_parts = plain_dot(activated_low, down_full).astype(LOW).reshape(GROUP, rows, width)
    feed = links.group_sum([feed_parts[r] for r in range(GROUP)])
    block_out = (middle + feed + bias_down).astype(LOW)
    grad_middle = grad_out + norm_back(grad_hidden_two, normed_two, inverse_two, gain_two)
    grad_branch = grad_middle.astype(LOW)
    grad_mixed_own = right_dot(grad_branch, out_full).astype(LOW)
    sent = [
        lax.dynamic_slice_in_dim(grad_mixed_own, (place ^ r) * shard, shard, 1)
        for r in range(GROUP)
    ]
    grad_mixed = jnp.concatenate(links.exchange(sent), axis=0)
    grad_packed = attention_back(packed, grad_mixed, allowed)
    grad_hidden_parts = right_dot(grad_packed, qkv_full).astype(LOW).reshape(GROUP, rows, width)
    grad_hidden_one = links.group_sum([grad_hidden_parts[r] for r in range(GROUP)])
    normed_one, inverse_one = norm_rows(token_rows)
    grad_inputs = grad_middle + norm_back(grad_hidden_one, normed_one, inverse_one, gain_one)

    def to_rows(full):
        columns = full.shape[1]
        chunks = full.astype(LOW).reshape(planes, GROUP, own_rows, columns)
        summed = links.plane_sum(chunks).astype(LOW)
        sent = [lax.dynamic_index_in_dim(summed, place ^ r, 0, False) for r in range(GROUP)]
        result = jnp.zeros((GROUP, own_rows, columns), LOW)
        for r, piece in enumerate(links.exchange(sent)):
            result = lax.dynamic_update_index_in_dim(result, piece, place ^ r, 0)
        return result.astype(WIDE)

    grad_down_w = links.plane_sum(
        left_dot(activated_low, grad_feed).astype(LOW).reshape(planes, own_hidden, width)
    )
    grad_up_w = to_rows(left_dot(hidden_two, grad_pre_low))
    grad_up_w = grad_up_w.reshape(GROUP, own_rows, planes, own_hidden).transpose(1, 2, 0, 3)
    grad_up_w = grad_up_w.reshape(own_rows, hidden)
    out_parts = left_dot(mixed, grad_branch).astype(LOW)
    out_parts = out_parts.reshape(planes, GROUP, own_rows, width)
    out_sum = links.group_sum(
        [lax.dynamic_index_in_dim(out_parts, place ^ r, 1, False) for r in range(GROUP)]
    )
    grad_out_w = links.plane_sum(out_sum.astype(LOW))
    grad_proj_w = to_rows(left_dot(hidden_one, grad_packed))
    grad_proj_w = grad_proj_w.reshape(GROUP, own_rows, 3, shard).transpose(1, 2, 0, 3)
    grad_proj_w = grad_proj_w.reshape(own_rows, 3 * width)

    packed_sums = jnp.sum(grad_packed.astype(WIDE), axis=0)
    proj_sums = jnp.zeros((2, width), WIDE)
    proj_sums = lax.dynamic_update_slice_in_dim(
        proj_sums,
        jnp.stack([packed_sums[:shard], packed_sums[2 * shard :]]),
        place * shard,
        1,
    )
    up_sums = jnp.zeros((planes, GROUP, own_hidden), WIDE)
    up_sums = lax.dynamic_update_index_in_dim(
        up_sums,
        jnp.sum(grad_pre_low.astype(WIDE), axis=0).reshape(planes, own_hidden),
        place,
        1,
    )
    vectors = [
        jnp.sum(grad_hidden_one * normed_one, axis=0),
        jnp.sum(grad_hidden_one, axis=0),
        jnp.sum(grad_branch.astype(WIDE), axis=0),
        jnp.sum(grad_hidden_two * normed_two, axis=0),
        jnp.sum(grad_hidden_two, axis=0),
        jnp.sum(grad_feed_own.astype(WIDE), axis=0),
        proj_sums,
        up_sums,
    ]
    vectors = jnp.concatenate([v.reshape(planes, GROUP, -1) for v in vectors], axis=2)
    sent = [lax.dynamic_index_in_dim(vectors, place ^ r, 1, False) for r in range(GROUP)]
    sums = links.plane_sum(sum(links.exchange(sent)))
    grads = [sums[i * own_rows : (i + 1) * own_rows] for i in range(6)]
    grad_proj_b = sums[6 * own_rows : 8 * own_rows]
    grad_up_b = sums[8 * own_rows :]
    return (
        block_out,
        grad_inputs,
        grads[0],
        grads[1],
        grad_proj_w,
        grad_proj_b,
        grad_out_w,
        grads[2],
        grads[3],
        grads[4],
        grad_up_w,
        grad_up_b,
        grad_down_w,
        grads[5],
    )


def solution(mesh):
    flat, wide = P("dp"), P("dp", None)
    in_specs = (
        (wide, flat, flat, flat, flat, wide, flat, wide, flat, flat, flat, wide, flat, wide)
        + (flat, wide)
    )
    out_specs = (
        (wide, wide, flat, flat, wide, flat, wide, flat, flat, flat, wide, flat, wide, flat)
    )
    return jax.shard_map(local, mesh=mesh, in_specs=in_specs, out_specs=out_specs, check_vma=False)
```

```python
import functools
import math

import jax
import jax.numpy as jnp
from jax import lax
from jax.experimental import pallas as pl
from jax.experimental.pallas import tpu as pltpu
from jax.sharding import PartitionSpec as P

HEAD_DIM = 64
EPS = 1e-05
NEG = -1e30
GROUP = 8
DIRECT_PLANES = 8
LOW = jnp.bfloat16
WIDE = jnp.float32


def norm_rows(inputs):
    average = jnp.mean(inputs, axis=-1, keepdims=True)
    centered = inputs - average
    variance = jnp.mean(centered * centered, axis=-1, keepdims=True)
    inverse = lax.rsqrt(variance + EPS)
    return (centered * inverse, inverse)


def norm_back(grad_in, normed, inverse, gain):
    scaled = grad_in * gain
    return inverse * (
        scaled
        - jnp.mean(scaled, axis=1, keepdims=True)
        - normed * jnp.mean(scaled * normed, axis=1, keepdims=True)
    )


def gelu_tanh(inputs):
    return (
        0.5
        * inputs
        * (1.0 + jnp.tanh(0.7978845608028654 * (inputs + 0.044715 * inputs * inputs * inputs)))
    )


def dot(first, second, dims):
    return lax.dot_general(first, second, (dims, ((), ())), preferred_element_type=jnp.float32)


def plain_dot(first, second):
    return dot(first, second, ((1,), (0,)))


def left_dot(first, second):
    return dot(first, second, ((0,), (0,)))


def right_dot(first, second):
    return dot(first, second, ((1,), (1,)))


def head_masks():
    lane = lax.broadcasted_iota(jnp.int32, (1, 2 * HEAD_DIM), 1)
    return [((lane // HEAD_DIM) == h).astype(LOW) for h in range(2)]


def softmax_rows(query, key, allowed):
    scores = right_dot(query, key) * (1.0 / math.sqrt(HEAD_DIM))
    scores = jnp.where(allowed, scores, NEG)
    top = jnp.max(scores, axis=1, keepdims=True)
    raw = jnp.exp(scores - top)
    return raw / jnp.sum(raw, axis=1, keepdims=True)


def attention_kernel(packed_ref, allowed_ref, out_ref):
    masks = head_masks()
    rows = allowed_ref.shape[1]
    width = 2 * HEAD_DIM
    for block in range(allowed_ref.shape[0]):
        part = pl.ds(block * rows, rows)
        query = packed_ref[part, :width]
        key = packed_ref[part, width : 2 * width]
        value = packed_ref[part, 2 * width :]
        allowed = allowed_ref[block] > 0
        total = None
        for mask in masks:
            weights = softmax_rows(query * mask, key, allowed).astype(LOW)
            term = plain_dot(weights, value * mask)
            total = term if total is None else total + term
        out_ref[part, :] = total.astype(LOW)


def attention_back_kernel(packed_ref, grad_ref, allowed_ref, out_ref):
    masks = head_masks()
    rows = allowed_ref.shape[1]
    width = 2 * HEAD_DIM
    scale = 1.0 / math.sqrt(HEAD_DIM)
    for block in range(allowed_ref.shape[0]):
        part = pl.ds(block * rows, rows)
        query = packed_ref[part, :width]
        key = packed_ref[part, width : 2 * width]
        value = packed_ref[part, 2 * width :]
        grad = grad_ref[part, :]
        allowed = allowed_ref[block] > 0
        sums = [None, None, None]
        for mask in masks:
            query_head = query * mask
            grad_head = grad * mask
            weights = softmax_rows(query_head, key, allowed)
            grad_weights = right_dot(grad_head, value)
            grad_scores = weights * (
                grad_weights - jnp.sum(grad_weights * weights, axis=1, keepdims=True)
            )
            grad_scores = grad_scores.astype(LOW)
            terms = (
                plain_dot(grad_scores, key * mask),
                left_dot(grad_scores, query_head),
                left_dot(weights.astype(LOW), grad_head),
            )
            sums = [t if s is None else s + t for s, t in zip(sums, terms)]
        out_ref[part, :width] = (sums[0] * scale).astype(LOW)
        out_ref[part, width : 2 * width] = (sums[1] * scale).astype(LOW)
        out_ref[part, 2 * width :] = sums[2].astype(LOW)


def block_place(i, place_ref):
    return place_ref[0] ^ (((i & 3) << 1) | (i >> 2))


def attention(packed, allowed, place):
    blocks, rows, _ = allowed.shape
    width = 2 * HEAD_DIM
    return pl.pallas_call(
        lambda place_ref, *refs: attention_kernel(*refs),
        grid_spec=pltpu.PrefetchScalarGridSpec(
            num_scalar_prefetch=1,
            grid=(blocks,),
            in_specs=[
                pl.BlockSpec((rows, 3 * width), lambda i, p: (i, 0)),
                pl.BlockSpec((1, rows, rows), lambda i, p: (block_place(i, p), 0, 0)),
            ],
            out_specs=pl.BlockSpec((rows, width), lambda i, p: (block_place(i, p), 0)),
        ),
        out_shape=jax.ShapeDtypeStruct((blocks * rows, width), LOW),
        cost_estimate=pl.CostEstimate(
            flops=8 * blocks * rows * rows * width,
            bytes_accessed=2 * packed.size + 4 * allowed.size,
            transcendentals=2 * allowed.size,
        ),
    )(place[None], packed, allowed)


def attention_back(packed, grad, allowed, place):
    blocks, rows, _ = allowed.shape
    width = 2 * HEAD_DIM
    return pl.pallas_call(
        lambda place_ref, *refs: attention_back_kernel(*refs),
        grid_spec=pltpu.PrefetchScalarGridSpec(
            num_scalar_prefetch=1,
            grid=(blocks,),
            in_specs=[
                pl.BlockSpec((rows, 3 * width), lambda i, p: (i, 0)),
                pl.BlockSpec((rows, width), lambda i, p: (block_place(i, p), 0)),
                pl.BlockSpec((1, rows, rows), lambda i, p: (block_place(i, p), 0, 0)),
            ],
            out_specs=pl.BlockSpec((rows, 3 * width), lambda i, p: (i, 0)),
        ),
        out_shape=jax.ShapeDtypeStruct((blocks * rows, 3 * width), LOW),
        cost_estimate=pl.CostEstimate(
            flops=20 * blocks * rows * rows * width,
            bytes_accessed=4 * packed.size + 4 * allowed.size,
            transcendentals=2 * allowed.size,
        ),
    )(place[None], packed, grad, allowed)


class Links:
    def __init__(self, count):
        self.count = count
        self.planes = count // GROUP
        index = lax.axis_index("dp")
        self.place = index & (GROUP - 1)
        self.plane = index // GROUP

    def swap(self, array, flip):
        return lax.ppermute(array, "dp", [(i, i ^ flip) for i in range(self.count)])

    def shift(self, array, steps):
        hop = steps * GROUP
        return lax.ppermute(array, "dp", [(i, (i + hop) % self.count) for i in range(self.count)])

    def chip_gather(self, block):
        others = {flip: self.swap(block, flip) for flip in (6, 2, 4)}
        return jnp.concatenate([block, others[2], others[4], others[6]], axis=0)

    def core_gather(self, near):
        return jnp.concatenate([near, self.swap(near, 1)], axis=0)

    def core_sum(self, near, far):
        return (near.astype(WIDE) + self.swap(far, 1).astype(WIDE)).astype(LOW)

    def chip_sum(self, halves):
        total = halves[0].astype(WIDE)
        for k in (3, 1, 2):
            total = total + self.swap(halves[k], 2 * k).astype(WIDE)
        return total

    def group_lists(self):
        return [[p * GROUP + j for j in range(GROUP)] for p in range(self.planes)]

    def plane_exchange(self, parts):
        return lax.all_to_all(
            parts, "dp", 0, 0, axis_index_groups=self.plane_groups(), tiled=True
        )

    def exchange(self, parts):
        return lax.all_to_all(
            parts, "dp", 0, 0, axis_index_groups=self.group_lists(), tiled=True
        )

    def plane_groups(self):
        return [[p * GROUP + j for p in range(self.planes)] for j in range(GROUP)]

    def plane_gather(self, block):
        if self.planes > DIRECT_PLANES:
            return lax.all_gather(block, "dp", axis_index_groups=self.plane_groups())
        found = jnp.zeros((self.planes,) + block.shape, block.dtype)
        found = lax.dynamic_update_index_in_dim(found, block, self.plane, 0)
        for k in range(1, self.planes):
            source = (self.plane + self.planes - k) % self.planes
            found = lax.dynamic_update_index_in_dim(found, self.shift(block, k), source, 0)
        return found

    def plane_sum(self, chunks):
        if self.planes > DIRECT_PLANES:
            return lax.psum_scatter(
                chunks.astype(WIDE), "dp", axis_index_groups=self.plane_groups()
            )
        total = lax.dynamic_index_in_dim(chunks, self.plane, 0, False).astype(WIDE)
        for k in range(1, self.planes):
            target = (self.plane + k) % self.planes
            term = lax.dynamic_index_in_dim(chunks, target, 0, False)
            total = total + self.shift(term, k).astype(WIDE)
        return total


def after(array, *others):
    return lax.optimization_barrier((array,) + others)[0]


def local(
    tokens,
    segment_ids,
    pad_mask,
    ln1_gain,
    ln1_bias,
    qkv_weight,
    qkv_bias,
    out_weight,
    out_bias,
    ln2_gain,
    ln2_bias,
    up_weight,
    up_bias,
    down_weight,
    down_bias,
    cotangent,
):
    count = lax.axis_size("dp")
    links = Links(count)
    place, planes = links.place, links.planes
    rows, width = tokens.shape
    own_rows = qkv_weight.shape[0]
    hidden = up_weight.shape[1]
    shard = width // GROUP
    hidden_shard = hidden // GROUP
    own_hidden = hidden // count
    heads_width = 3 * shard

    code = (segment_ids * 2 + pad_mask).astype(LOW)
    fill = jnp.zeros((shard - 4 * own_rows,), LOW)
    wide_fill = jnp.zeros((shard - own_hidden,), LOW)
    empty = jnp.zeros((shard,), LOW)
    small = [
        jnp.concatenate([ln1_gain, ln1_bias, out_bias, ln2_gain, fill]),
        jnp.concatenate([ln2_bias, down_bias, qkv_bias, fill]),
        jnp.concatenate([up_bias, wide_fill]),
        code,
    ]
    small = jnp.stack(small + [empty] * 4)
    qkv_parts = qkv_weight.reshape(own_rows, 3, GROUP, shard).transpose(2, 1, 0, 3)
    qkv_parts = qkv_parts.reshape(GROUP, 3 * own_rows, shard)
    small_parts = jnp.broadcast_to(small[None], (GROUP,) + small.shape)
    sent = jnp.concatenate([qkv_parts, small_parts], axis=1)
    sent = jnp.broadcast_to(sent[None], (planes,) + sent.shape).reshape((count,) + sent.shape[1:])
    up_parts = up_weight.reshape(own_rows, planes, GROUP, own_hidden)
    up_parts = up_parts.transpose(2, 0, 1, 3).reshape(GROUP, own_rows, hidden_shard)
    up_plane = links.exchange(up_parts)
    sent = after(sent, up_plane)
    token_near = links.chip_gather(tokens)
    up_full = links.plane_gather(up_plane).reshape(width, hidden_shard)
    buffer = lax.all_to_all(sent, "dp", 0, 0, tiled=True)
    buffer, token_near = lax.optimization_barrier((buffer, token_near))
    out_full = lax.all_gather(out_weight, "dp", axis=0, tiled=True)
    down_full = lax.all_gather(
        down_weight, "dp", axis_index_groups=links.plane_groups(), tiled=True
    )
    qkv_full = jnp.concatenate(
        [
            buffer[:, i * own_rows : (i + 1) * own_rows].reshape(width, shard)
            for i in range(3)
        ],
        axis=1,
    )

    def small_vector(row, start, length):
        start = start * own_rows
        return buffer[:, 3 * own_rows + row, start : start + length].astype(WIDE)

    gain_one, bias_one, bias_out, gain_two, bias_two, bias_down = (
        small_vector(i // 4, i % 4, own_rows).reshape(width) for i in range(6)
    )
    qkv_bias_all = small_vector(1, 2, 2 * own_rows).reshape(2, width)
    bias_qv = lax.dynamic_slice_in_dim(qkv_bias_all, place * shard, shard, 1)
    bias_heads = jnp.concatenate([bias_qv[0], jnp.zeros((shard,), WIDE), bias_qv[1]])
    up_bias_all = small_vector(2, 0, own_hidden).reshape(planes, GROUP, own_hidden)
    bias_up = lax.dynamic_index_in_dim(up_bias_all, place, 1, False).reshape(hidden_shard)

    token_all = links.core_gather(token_near)
    codes = lax.dynamic_slice_in_dim(small_vector(3, 0, rows), links.plane * GROUP, GROUP, 0)
    codes = codes.astype(jnp.int32)
    segments, live = codes >> 1, codes & 1
    positions = jnp.arange(rows, dtype=jnp.int32)
    allowed = (
        (segments[:, :, None] == segments[:, None, :])
        & (positions[None, :] <= positions[:, None])[None]
        & (live[:, None, :] == 1)
    ).astype(WIDE)

    grad_out = cotangent.astype(WIDE) * pad_mask.astype(WIDE)[:, None]
    grad_feed_own = grad_out.astype(LOW)

    normed_all, _ = norm_rows(token_all.astype(WIDE))
    hidden_one = (normed_all * gain_one + bias_one).astype(LOW)
    packed = (plain_dot(hidden_one, qkv_full) + bias_heads).astype(LOW)
    grad_feed_near = links.chip_gather(after(grad_feed_own, packed))
    mixed_heads = attention(packed, allowed, place).reshape(GROUP, rows, shard)
    mixed = links.exchange(after(mixed_heads, grad_feed_near))
    grad_feed = links.core_gather(after(grad_feed_near, mixed_heads))
    mixed = mixed.transpose(1, 0, 2).reshape(rows, width)
    token_rows = tokens.astype(WIDE)
    middle = token_rows + (plain_dot(mixed, out_full) + bias_out)
    normed_two, inverse_two = norm_rows(middle)
    hidden_two_own = (normed_two * gain_two + bias_two).astype(LOW)
    hidden_two_near = links.chip_gather(hidden_two_own)
    hidden_two = links.core_gather(after(hidden_two_near, up_full, grad_feed))
    pre_act = plain_dot(hidden_two, up_full) + bias_up
    activated, gelu_pull = jax.vjp(gelu_tanh, pre_act)
    activated_low = activated.astype(LOW)

    (grad_pre,) = gelu_pull(right_dot(grad_feed, down_full))
    grad_pre_low = grad_pre.astype(LOW)
    half_rows = GROUP * rows // 2
    far = right_dot(grad_pre_low[half_rows:], up_full).astype(LOW)
    near = right_dot(grad_pre_low[:half_rows], up_full).astype(LOW)
    grad_hidden_half = links.core_sum(near, far).reshape(4, rows, width)
    grad_hidden_two = links.chip_sum(grad_hidden_half)
    activated_low, _ = lax.optimization_barrier((activated_low, grad_hidden_half))
    far = plain_dot(activated_low[half_rows:], down_full).astype(LOW)
    near = plain_dot(activated_low[:half_rows], down_full).astype(LOW)
    feed_half = links.core_sum(near, far).reshape(4, rows, width)
    grad_middle = grad_out + norm_back(grad_hidden_two, normed_two, inverse_two, gain_two)
    grad_branch = grad_middle.astype(LOW)
    grad_mixed_own = right_dot(grad_branch, out_full).astype(LOW)
    grad_mixed = links.exchange(grad_mixed_own.reshape(rows, GROUP, shard).transpose(1, 0, 2))
    grad_mixed = grad_mixed.reshape(GROUP * rows, shard)

    out_parts = left_dot(mixed, grad_branch).astype(LOW)
    out_parts = out_parts.reshape(planes, GROUP, own_rows, width)
    near, far = (
        jnp.stack(
            [lax.dynamic_index_in_dim(out_parts, place ^ r, 1, False) for r in order]
        ).reshape(4, planes * own_rows, width)
        for order in ((0, 2, 4, 6), (1, 3, 5, 7))
    )
    out_half = links.core_sum(near, far)
    both_half = jnp.concatenate([feed_half, out_half], axis=1)
    both_sum = links.chip_sum(both_half)
    feed, out_sum = both_sum[:rows], both_sum[rows:].astype(LOW)
    block_out = (middle + feed + bias_down).astype(LOW)

    hidden_two, activated_low, _ = lax.optimization_barrier(
        (hidden_two, activated_low, grad_mixed_own)
    )
    pieces = [left_dot(hidden_two, grad_pre_low).astype(LOW).reshape(planes, -1, hidden_shard)]
    for start in range(0, width, hidden_shard):
        piece = left_dot(activated_low, grad_feed[:, start : start + hidden_shard]).astype(LOW)
        pieces.append(piece.reshape(planes, own_hidden, hidden_shard))
    both_rows = lax.psum_scatter(
        jnp.concatenate(pieces, axis=1), "dp", axis_index_groups=links.plane_groups()
    )
    up_rows = both_rows[: GROUP * own_rows].reshape(GROUP, own_rows, hidden_shard)
    grad_down_w = both_rows[GROUP * own_rows :].reshape(-1, own_hidden, hidden_shard)
    grad_down_w = grad_down_w.transpose(1, 0, 2).reshape(own_hidden, width).astype(WIDE)

    grad_packed = attention_back(packed, after(grad_mixed, both_half), allowed, place)
    far = right_dot(grad_packed[half_rows:], qkv_full).astype(LOW)
    near = right_dot(grad_packed[:half_rows], qkv_full).astype(LOW)
    grad_hidden_half = links.core_sum(near, far).reshape(4, rows, width)
    grad_hidden_one = links.chip_sum(after(grad_hidden_half, both_sum))
    normed_one, inverse_one = norm_rows(token_rows)
    grad_inputs = grad_middle + norm_back(grad_hidden_one, normed_one, inverse_one, gain_one)

    proj_rows = left_dot(hidden_one, grad_packed).astype(LOW)
    proj_rows = proj_rows.reshape(planes, GROUP, own_rows, heads_width)
    proj_rows = links.plane_sum(proj_rows).astype(LOW)
    grad_out_w = links.plane_exchange(out_sum.reshape(planes, own_rows, width))
    grad_out_w = jnp.sum(grad_out_w.astype(WIDE), axis=0)
    row_blocks = links.exchange(jnp.concatenate([proj_rows, up_rows], axis=2)).astype(WIDE)
    grad_proj_w = row_blocks[:, :, :heads_width]
    grad_proj_w = grad_proj_w.reshape(GROUP, own_rows, 3, shard).transpose(1, 2, 0, 3)
    grad_proj_w = grad_proj_w.reshape(own_rows, 3 * width)
    grad_up_w = row_blocks[:, :, heads_width:]
    grad_up_w = grad_up_w.reshape(GROUP, own_rows, planes, own_hidden).transpose(1, 2, 0, 3)
    grad_up_w = grad_up_w.reshape(own_rows, hidden)

    packed_sums = jnp.sum(grad_packed.astype(WIDE), axis=0)
    proj_sums = jnp.zeros((2, width), WIDE)
    proj_sums = lax.dynamic_update_slice_in_dim(
        proj_sums,
        jnp.stack([packed_sums[:shard], packed_sums[2 * shard :]]),
        place * shard,
        1,
    )
    up_sums = jnp.zeros((planes, GROUP, own_hidden), WIDE)
    up_sums = lax.dynamic_update_index_in_dim(
        up_sums,
        jnp.sum(grad_pre_low.astype(WIDE), axis=0).reshape(planes, own_hidden),
        place,
        1,
    )
    def over_tokens(scale):
        terms = ((near, normed_all[:half_rows]), (far, normed_all[half_rows:]))
        return sum(
            jnp.sum(part.astype(WIDE) * (normed if scale else 1.0), axis=0)
            for part, normed in terms
        )

    vectors = [
        over_tokens(True),
        over_tokens(False),
        jnp.sum(grad_branch.astype(WIDE), axis=0),
        jnp.sum(grad_hidden_two * normed_two, axis=0),
        jnp.sum(grad_hidden_two, axis=0),
        jnp.sum(grad_feed_own.astype(WIDE), axis=0),
        proj_sums,
        up_sums,
    ]
    vectors = jnp.concatenate([v.reshape(planes, GROUP, -1) for v in vectors], axis=2)
    vectors = vectors.reshape(count, -1)
    sums = jnp.sum(lax.all_to_all(vectors, "dp", 0, 0, tiled=True), axis=0)
    grads = [sums[i * own_rows : (i + 1) * own_rows] for i in range(6)]
    grad_proj_b = sums[6 * own_rows : 8 * own_rows]
    grad_up_b = sums[8 * own_rows :]
    return (
        block_out,
        grad_inputs,
        grads[0],
        grads[1],
        grad_proj_w,
        grad_proj_b,
        grad_out_w,
        grads[2],
        grads[3],
        grads[4],
        grad_up_w,
        grad_up_b,
        grad_down_w,
        grads[5],
    )


def solution(mesh):
    flat, wide = P("dp"), P("dp", None)
    in_specs = (
        (wide, flat, flat, flat, flat, wide, flat, wide, flat, flat, flat, wide, flat, wide)
        + (flat, wide)
    )
    out_specs = (
        (wide, wide, flat, flat, wide, flat, wide, flat, flat, flat, wide, flat, wide, flat)
    )
    return jax.shard_map(local, mesh=mesh, in_specs=in_specs, out_specs=out_specs, check_vma=False)
```

```python
import functools
import math

import jax
import jax.numpy as jnp
from jax import lax
from jax.experimental import pallas as pl
from jax.experimental.pallas import tpu as pltpu
from jax.sharding import PartitionSpec as P

HEAD_DIM = 64
EPS = 1e-05
NEG = -1e30
GROUP = 8
DIRECT_PLANES = 8
VMEM_BYTES = 56 << 20
LOW = jnp.bfloat16
WIDE = jnp.float32


def norm_rows(inputs):
    average = jnp.mean(inputs, axis=-1, keepdims=True)
    centered = inputs - average
    variance = jnp.mean(centered * centered, axis=-1, keepdims=True)
    inverse = lax.rsqrt(variance + EPS)
    return (centered * inverse, inverse)


def norm_back(grad_in, normed, inverse, gain):
    scaled = grad_in * gain
    return inverse * (
        scaled
        - jnp.mean(scaled, axis=1, keepdims=True)
        - normed * jnp.mean(scaled * normed, axis=1, keepdims=True)
    )


def gelu_tanh(inputs):
    return (
        0.5
        * inputs
        * (1.0 + jnp.tanh(0.7978845608028654 * (inputs + 0.044715 * inputs * inputs * inputs)))
    )


def dot(first, second, dims):
    return lax.dot_general(first, second, (dims, ((), ())), preferred_element_type=jnp.float32)


def plain_dot(first, second):
    return dot(first, second, ((1,), (0,)))


def left_dot(first, second):
    return dot(first, second, ((0,), (0,)))


def right_dot(first, second):
    return dot(first, second, ((1,), (1,)))


def head_masks():
    lane = lax.broadcasted_iota(jnp.int32, (1, 2 * HEAD_DIM), 1)
    return [((lane // HEAD_DIM) == h).astype(LOW) for h in range(2)]


def softmax_rows(query, key, allowed):
    scores = right_dot(query, key) * (1.0 / math.sqrt(HEAD_DIM))
    scores = jnp.where(allowed, scores, NEG)
    top = jnp.max(scores, axis=1, keepdims=True)
    raw = jnp.exp(scores - top)
    return raw / jnp.sum(raw, axis=1, keepdims=True)


def pick_block(step, refs, target_ref):
    for k, ref in enumerate(refs):

        @pl.when(step == k)
        def _(ref=ref):
            target_ref[...] = ref[...]


def attention_kernel(place_ref, *refs):
    token_refs, refs = refs[:GROUP], refs[GROUP:]
    gain_ref, offset_ref, bias_ref, pieces_ref, allowed_ref, *refs = refs
    hidden_ref, normed_ref, packed_ref, weight_ref, out_ref, block_ref = refs
    step = pl.program_id(0)
    width = 2 * HEAD_DIM
    own_rows = weight_ref.shape[0] // pieces_ref.shape[0]

    @pl.when(step == 0)
    def _():
        for part in range(3):
            piece = pieces_ref[:, part * own_rows : (part + 1) * own_rows, :]
            weight_ref[:, part * width : (part + 1) * width] = piece.reshape(-1, width)

    pick_block(step, token_refs, block_ref)
    normed, _ = norm_rows(block_ref[...].astype(WIDE))
    hidden = (normed * gain_ref[...] + offset_ref[...]).astype(LOW)
    normed_ref[...] = normed.astype(LOW)
    hidden_ref[...] = hidden
    packed = (plain_dot(hidden, weight_ref[...]) + bias_ref[...]).astype(LOW)
    packed_ref[...] = packed
    key, value = packed[:, width : 2 * width], packed[:, 2 * width :]
    allowed = allowed_ref[0] > 0
    total = None
    for mask in head_masks():
        weights = softmax_rows(packed[:, :width] * mask, key, allowed).astype(LOW)
        term = plain_dot(weights, value * mask)
        total = term if total is None else total + term
    out_ref[...] = total.astype(LOW)


def attention_back_kernel(
    packed_ref,
    grad_ref,
    allowed_ref,
    weight_ref,
    normed_ref,
    out_ref,
    near_ref,
    far_ref,
    norm_sums_ref,
    bias_sums_ref,
):
    masks = head_masks()
    rows = allowed_ref.shape[1]
    width = 2 * HEAD_DIM
    scale = 1.0 / math.sqrt(HEAD_DIM)
    for block in range(allowed_ref.shape[0]):
        part = pl.ds(block * rows, rows)
        query = packed_ref[part, :width]
        key = packed_ref[part, width : 2 * width]
        value = packed_ref[part, 2 * width :]
        grad = grad_ref[part, :]
        allowed = allowed_ref[block] > 0
        sums = [None, None, None]
        for mask in masks:
            query_head = query * mask
            grad_head = grad * mask
            weights = softmax_rows(query_head, key, allowed)
            grad_weights = right_dot(grad_head, value)
            grad_scores = weights * (
                grad_weights - jnp.sum(grad_weights * weights, axis=1, keepdims=True)
            )
            grad_scores = grad_scores.astype(LOW)
            terms = (
                plain_dot(grad_scores, key * mask),
                left_dot(grad_scores, query_head),
                left_dot(weights.astype(LOW), grad_head),
            )
            sums = [t if s is None else s + t for s, t in zip(sums, terms)]
        out_ref[part, :width] = (sums[0] * scale).astype(LOW)
        out_ref[part, width : 2 * width] = (sums[1] * scale).astype(LOW)
        out_ref[part, 2 * width :] = sums[2].astype(LOW)
    grad_hidden = right_dot(out_ref[...], weight_ref[...])
    hidden = grad_hidden.astype(LOW)
    step = pl.program_id(0)
    gain_sums = jnp.sum(grad_hidden * normed_ref[...].astype(WIDE), axis=0, keepdims=True)
    plain_sums = jnp.sum(grad_hidden, axis=0, keepdims=True)
    norm_sums = jnp.concatenate([gain_sums, plain_sums], axis=0)
    bias_sums = jnp.sum(out_ref[...].astype(WIDE), axis=0, keepdims=True)

    @pl.when(step == 0)
    def _():
        norm_sums_ref[...] = norm_sums
        bias_sums_ref[...] = bias_sums

    @pl.when(step > 0)
    def _():
        norm_sums_ref[...] += norm_sums
        bias_sums_ref[...] += bias_sums

    @pl.when(step < pl.num_programs(0) // 2)
    def _():
        near_ref[...] = hidden

    @pl.when(step >= pl.num_programs(0) // 2)
    def _():
        far_ref[...] = hidden


def block_place(i, place_ref):
    return place_ref[0] ^ (((i & 3) << 1) | (i >> 2))


def fixed(shape):
    return pl.BlockSpec(shape, lambda i, p: (0,) * len(shape))


def attention(blocks, gain, offset, bias, pieces, allowed, places):
    rows, model_width = blocks[0].shape
    width = 2 * HEAD_DIM
    count = len(blocks)
    return pl.pallas_call(
        attention_kernel,
        grid_spec=pltpu.PrefetchScalarGridSpec(
            num_scalar_prefetch=1,
            grid=(count,),
            in_specs=[fixed((rows, model_width))] * count
            + [
                fixed((1, model_width)),
                fixed((1, model_width)),
                fixed((1, 3 * width)),
                fixed(pieces.shape),
                pl.BlockSpec((1, rows, rows), lambda i, p: (block_place(i, p), 0, 0)),
            ],
            out_specs=[
                pl.BlockSpec((rows, model_width), lambda i, p: (i, 0)),
                pl.BlockSpec((rows, model_width), lambda i, p: (i, 0)),
                pl.BlockSpec((rows, 3 * width), lambda i, p: (i, 0)),
                fixed((model_width, 3 * width)),
                pl.BlockSpec((rows, width), lambda i, p: (block_place(i, p), 0)),
            ],
            scratch_shapes=[pltpu.VMEM((rows, model_width), LOW)],
        ),
        out_shape=[
            jax.ShapeDtypeStruct((count * rows, model_width), LOW),
            jax.ShapeDtypeStruct((count * rows, model_width), LOW),
            jax.ShapeDtypeStruct((count * rows, 3 * width), LOW),
            jax.ShapeDtypeStruct((model_width, 3 * width), LOW),
            jax.ShapeDtypeStruct((count * rows, width), LOW),
        ],
        compiler_params=pltpu.CompilerParams(vmem_limit_bytes=VMEM_BYTES),
        cost_estimate=pl.CostEstimate(
            flops=8 * count * rows * rows * width,
            bytes_accessed=count * rows * model_width,
            transcendentals=0,
        ),
    )(places, *blocks, gain, offset, bias, pieces, allowed)


def attention_back(packed, grad, allowed, weight, normed, places, earlier):
    blocks, rows, _ = allowed.shape
    width = 2 * HEAD_DIM
    model_width = weight.shape[0]
    half = blocks // 2
    return pl.pallas_call(
        lambda place_ref, a_ref, *refs: attention_back_kernel(*refs),
        grid_spec=pltpu.PrefetchScalarGridSpec(
            num_scalar_prefetch=1,
            grid=(blocks,),
            in_specs=[
                pl.BlockSpec(memory_space=pl.ANY),
                pl.BlockSpec((rows, 3 * width), lambda i, p: (i, 0)),
                pl.BlockSpec((rows, width), lambda i, p: (block_place(i, p), 0)),
                pl.BlockSpec((1, rows, rows), lambda i, p: (block_place(i, p), 0, 0)),
                pl.BlockSpec((model_width, 3 * width), lambda i, p: (0, 0)),
                pl.BlockSpec((rows, model_width), lambda i, p: (i, 0)),
            ],
            out_specs=[
                pl.BlockSpec((rows, 3 * width), lambda i, p: (i, 0)),
                pl.BlockSpec(
                    (rows, model_width), lambda i, p: ((p[0] >> 1) ^ jnp.minimum(i, half - 1), 0)
                ),
                pl.BlockSpec(
                    (rows, model_width),
                    lambda i, p: ((p[0] >> 1) ^ (jnp.maximum(i, half) - half), 0),
                ),
                pl.BlockSpec((2, model_width), lambda i, p: (0, 0)),
                pl.BlockSpec((1, 3 * width), lambda i, p: (0, 0)),
            ],
        ),
        out_shape=[
            jax.ShapeDtypeStruct((blocks * rows, 3 * width), LOW),
            jax.ShapeDtypeStruct((half * rows, model_width), LOW),
            jax.ShapeDtypeStruct((half * rows, model_width), LOW),
            jax.ShapeDtypeStruct((2, model_width), WIDE),
            jax.ShapeDtypeStruct((1, 3 * width), WIDE),
        ],
        compiler_params=pltpu.CompilerParams(vmem_limit_bytes=VMEM_BYTES),
        cost_estimate=pl.CostEstimate(
            flops=20 * blocks * rows * rows * width,
            bytes_accessed=4 * packed.size + 4 * allowed.size,
            transcendentals=2 * allowed.size,
        ),
    )(places, earlier, packed, grad, allowed, weight, normed)


def feed_kernel(place_ref, *refs):
    input_refs, grad_refs, refs = refs[:GROUP], refs[GROUP : 2 * GROUP], refs[2 * GROUP :]
    planes = len(refs) - 11
    up_refs, refs = refs[:planes], refs[planes:]
    down_ref, bias_ref, input_ref, grad_ref, act_ref, pre_ref, sums_ref, near_ref, far_ref = refs[:9]
    up_ref = refs[9]
    step = pl.program_id(0)
    rows = input_ref.shape[0] // 2
    pick_block(step, input_refs[0::2], input_ref.at[pl.ds(0, rows)])
    pick_block(step, input_refs[1::2], input_ref.at[pl.ds(rows, rows)])
    pick_block(step, grad_refs[0::2], grad_ref.at[pl.ds(0, rows)])
    pick_block(step, grad_refs[1::2], grad_ref.at[pl.ds(rows, rows)])

    @pl.when(step == 0)
    def _():
        for k, ref in enumerate(up_refs):
            depth = ref.shape[0] * ref.shape[1]
            source = lax.rem(place_ref[1] + planes - k, planes) * depth
            up_ref[pl.ds(pl.multiple_of(source, depth), depth), :] = ref[...].reshape(depth, -1)

    root, cube = 0.7978845608028654, 0.044715
    pre = plain_dot(input_ref[...], up_ref[...]) + bias_ref[...]
    square = pre * pre
    bend = jnp.tanh(root * (pre + cube * square * pre))
    act_ref[...] = (0.5 * pre * (1.0 + bend)).astype(LOW)
    slope = 0.5 * (1.0 + bend) + 0.5 * pre * (1.0 - bend * bend) * (
        root * (1.0 + 3.0 * cube * square)
    )
    grad_pre = (right_dot(grad_ref[...], down_ref[...]) * slope).astype(LOW)
    pre_ref[...] = grad_pre
    sums = jnp.sum(grad_pre.astype(WIDE), axis=0, keepdims=True)

    @pl.when(step == 0)
    def _():
        sums_ref[...] = sums

    @pl.when(step > 0)
    def _():
        sums_ref[...] += sums

    hidden = right_dot(grad_pre, up_ref[...]).astype(LOW)
    odd = (place_ref[0] >> 1) & 1
    first = pl.ds(pl.multiple_of(odd * rows, rows), rows)
    second = pl.ds(pl.multiple_of((1 - odd) * rows, rows), rows)
    for ref, wanted in (
        (near_ref, step < pl.num_programs(0) // 2),
        (far_ref, step >= pl.num_programs(0) // 2),
    ):

        @pl.when(wanted)
        def _(ref=ref):
            ref[first, :] = hidden[:rows]
            ref[second, :] = hidden[rows:]


def feed_forward(inputs, grads, up_parts, down, bias, places):
    block_rows, width = inputs[0].shape
    hidden = down.shape[0]
    tokens = GROUP * block_rows
    rows = 2 * block_rows
    steps = tokens // rows
    half = steps // 2
    return pl.pallas_call(
        feed_kernel,
        grid_spec=pltpu.PrefetchScalarGridSpec(
            num_scalar_prefetch=1,
            grid=(steps,),
            in_specs=[fixed((block_rows, width))] * (2 * GROUP)
            + [fixed(part.shape) for part in up_parts]
            + [fixed((hidden, width)), fixed((1, hidden))],
            out_specs=[
                pl.BlockSpec((rows, width), lambda i, p: (i, 0)),
                pl.BlockSpec((rows, width), lambda i, p: (i, 0)),
                pl.BlockSpec((rows, hidden), lambda i, p: (i, 0)),
                pl.BlockSpec((rows, hidden), lambda i, p: (i, 0)),
                fixed((1, hidden)),
                pl.BlockSpec((rows, width), lambda i, p: ((p[0] >> 2) ^ jnp.minimum(i, half - 1), 0)),
                pl.BlockSpec(
                    (rows, width), lambda i, p: ((p[0] >> 2) ^ (jnp.maximum(i, half) - half), 0)
                ),
            ],
            scratch_shapes=[pltpu.VMEM((width, hidden), LOW), pltpu.SMEM((1,), jnp.int32)],
        ),
        out_shape=[
            jax.ShapeDtypeStruct((tokens, width), LOW),
            jax.ShapeDtypeStruct((tokens, width), LOW),
            jax.ShapeDtypeStruct((tokens, hidden), LOW),
            jax.ShapeDtypeStruct((tokens, hidden), LOW),
            jax.ShapeDtypeStruct((1, hidden), WIDE),
            jax.ShapeDtypeStruct((tokens // 2, width), LOW),
            jax.ShapeDtypeStruct((tokens // 2, width), LOW),
        ],
        compiler_params=pltpu.CompilerParams(vmem_limit_bytes=VMEM_BYTES),
        cost_estimate=pl.CostEstimate(
            flops=tokens * width * hidden,
            bytes_accessed=tokens * width,
            transcendentals=0,
        ),
    )(places, *inputs, *grads, *up_parts, down, bias)


class Links:
    def __init__(self, count):
        self.count = count
        self.planes = count // GROUP
        index = lax.axis_index("dp")
        self.place = index & (GROUP - 1)
        self.plane = index // GROUP

    def swap(self, array, flip):
        return lax.ppermute(array, "dp", [(i, i ^ flip) for i in range(self.count)])

    def shift(self, array, steps):
        hop = steps * GROUP
        return lax.ppermute(array, "dp", [(i, (i + hop) % self.count) for i in range(self.count)])

    def group_gather(self, block):
        near = [block] + [None] * 3
        for k in (3, 1, 2):
            near[k] = self.swap(block, 2 * k)
        far = [self.swap(b, 1) for b in near]
        return near + far

    def core_sum(self, near, far, order=0.0):
        return (near.astype(WIDE) + (self.swap(far, 1).astype(WIDE) + order)).astype(LOW)

    def chip_sum(self, halves):
        total = halves[0].astype(WIDE)
        for k in (3, 1, 2):
            total = total + self.swap(halves[k], 2 * k).astype(WIDE)
        return total

    def chip_exchange(self, halves):
        chips = GROUP // 2
        groups = [
            [p * GROUP + 2 * m + c for m in range(chips)]
            for p in range(self.planes)
            for c in range(2)
        ]
        parts = halves.reshape(chips, halves.shape[0] // chips, halves.shape[1])
        terms = lax.all_to_all(parts, "dp", 0, 0, axis_index_groups=groups, tiled=True)
        return jnp.sum(terms.astype(WIDE), axis=0)

    def group_lists(self):
        return [[p * GROUP + j for j in range(GROUP)] for p in range(self.planes)]

    def plane_exchange(self, parts):
        return lax.all_to_all(
            parts, "dp", 0, 0, axis_index_groups=self.plane_groups(), tiled=True
        )

    def exchange(self, parts):
        return lax.all_to_all(
            parts, "dp", 0, 0, axis_index_groups=self.group_lists(), tiled=True
        )

    def plane_groups(self):
        return [[p * GROUP + j for p in range(self.planes)] for j in range(GROUP)]

    def plane_gather(self, block):
        if self.planes > DIRECT_PLANES:
            found = lax.all_gather(block, "dp", axis_index_groups=self.plane_groups())
            return [
                lax.dynamic_index_in_dim(found, (self.plane - k) % self.planes, 0, False)
                for k in range(self.planes)
            ]
        return [block] + [self.shift(block, k) for k in range(1, self.planes)]

    def plane_sum(self, chunks):
        if self.planes > DIRECT_PLANES:
            return lax.psum_scatter(
                chunks.astype(WIDE), "dp", axis_index_groups=self.plane_groups()
            )
        total = lax.dynamic_index_in_dim(chunks, self.plane, 0, False).astype(WIDE)
        for k in range(1, self.planes):
            target = (self.plane + k) % self.planes
            term = lax.dynamic_index_in_dim(chunks, target, 0, False)
            total = total + self.shift(term, k).astype(WIDE)
        return total


def order_zero(array):
    return array[(0,) * array.ndim].astype(WIDE) * 0.0


def local(
    tokens,
    segment_ids,
    pad_mask,
    ln1_gain,
    ln1_bias,
    qkv_weight,
    qkv_bias,
    out_weight,
    out_bias,
    ln2_gain,
    ln2_bias,
    up_weight,
    up_bias,
    down_weight,
    down_bias,
    cotangent,
):
    count = lax.axis_size("dp")
    links = Links(count)
    place, planes = links.place, links.planes
    rows, width = tokens.shape
    own_rows = qkv_weight.shape[0]
    hidden = up_weight.shape[1]
    shard = width // GROUP
    hidden_shard = hidden // GROUP
    own_hidden = hidden // count
    heads_width = 3 * shard

    code = (segment_ids * 2 + pad_mask).astype(LOW)
    fill = jnp.zeros((shard - 4 * own_rows,), LOW)
    wide_fill = jnp.zeros((shard - own_hidden,), LOW)
    empty = jnp.zeros((shard,), LOW)
    small = [
        jnp.concatenate([ln1_gain, ln1_bias, out_bias, ln2_gain, fill]),
        jnp.concatenate([ln2_bias, down_bias, qkv_bias, fill]),
        jnp.concatenate([up_bias, wide_fill]),
        code,
    ]
    small = jnp.stack(small + [empty] * 4)
    qkv_parts = qkv_weight.reshape(own_rows, 3, GROUP, shard).transpose(2, 1, 0, 3)
    qkv_parts = qkv_parts.reshape(GROUP, 3 * own_rows, shard)
    small_parts = jnp.broadcast_to(small[None], (GROUP,) + small.shape)
    sent = jnp.concatenate([qkv_parts, small_parts], axis=1)
    sent = jnp.broadcast_to(sent[None], (planes,) + sent.shape).reshape((count,) + sent.shape[1:])
    up_parts = up_weight.reshape(own_rows, planes, GROUP, own_hidden)
    up_parts = up_parts.transpose(2, 0, 1, 3).reshape(GROUP, own_rows, hidden_shard)
    up_plane = links.exchange(up_parts)
    sent = sent + order_zero(up_plane).astype(LOW)
    token_blocks = links.group_gather(tokens)
    grad_out = cotangent.astype(WIDE) * pad_mask.astype(WIDE)[:, None]
    grad_feed_own = grad_out.astype(LOW)
    grad_feed_blocks = links.group_gather(grad_feed_own)
    buffer = lax.all_to_all(sent, "dp", 0, 0, tiled=True)
    out_full = lax.all_gather(out_weight, "dp", axis=0, tiled=True)
    down_full = lax.all_gather(
        down_weight, "dp", axis_index_groups=links.plane_groups(), tiled=True
    )
    def small_vector(row, start, length):
        start = start * own_rows
        return buffer[:, 3 * own_rows + row, start : start + length].astype(WIDE)

    gain_one, bias_one, bias_out, gain_two, bias_two, bias_down = (
        small_vector(i // 4, i % 4, own_rows).reshape(width) for i in range(6)
    )
    qkv_bias_all = small_vector(1, 2, 2 * own_rows).reshape(2, width)
    bias_qv = lax.dynamic_slice_in_dim(qkv_bias_all, place * shard, shard, 1)
    bias_heads = jnp.concatenate([bias_qv[0], jnp.zeros((shard,), WIDE), bias_qv[1]])
    up_bias_all = small_vector(2, 0, own_hidden).reshape(planes, GROUP, own_hidden)
    bias_up = lax.dynamic_index_in_dim(up_bias_all, place, 1, False).reshape(hidden_shard)

    codes = lax.dynamic_slice_in_dim(small_vector(3, 0, rows), links.plane * GROUP, GROUP, 0)
    codes = codes.astype(jnp.int32)
    segments, live = codes >> 1, codes & 1
    positions = jnp.arange(rows, dtype=jnp.int32)
    allowed = (
        (segments[:, :, None] == segments[:, None, :])
        & (positions[None, :] <= positions[:, None])[None]
        & (live[:, None, :] == 1)
    ).astype(WIDE)

    places = jnp.stack([place, links.plane])
    hidden_one, normed_low, packed, qkv_full, mixed_heads = attention(
        token_blocks,
        gain_one[None],
        bias_one[None],
        bias_heads[None],
        buffer,
        allowed,
        places,
    )
    up_blocks = links.plane_gather(up_plane)
    mixed_heads = mixed_heads.reshape(GROUP, rows, shard)
    mixed = links.exchange(mixed_heads)
    mixed = mixed.transpose(1, 0, 2).reshape(rows, width)
    token_rows = tokens.astype(WIDE)
    middle = token_rows + (plain_dot(mixed, out_full) + bias_out)
    normed_two, inverse_two = norm_rows(middle)
    hidden_two_own = (normed_two * gain_two + bias_two).astype(LOW)
    up_here = sum(order_zero(b) for b in up_blocks[1:])
    hidden_two_own = (hidden_two_own.astype(WIDE) + up_here).astype(LOW)
    hidden_two_blocks = links.group_gather(hidden_two_own)

    half_rows = GROUP * rows // 2
    hidden_two, grad_feed, activated_low, grad_pre_low, up_bias_sums, near, far = feed_forward(
        hidden_two_blocks, grad_feed_blocks, up_blocks, down_full, bias_up[None], places
    )
    grad_hidden_half = links.core_sum(near, far)
    grad_hidden_two = links.chip_exchange(grad_hidden_half)
    far = plain_dot(activated_low[half_rows:], down_full).astype(LOW)
    near = plain_dot(activated_low[:half_rows], down_full).astype(LOW)
    feed_near, feed_far = near, far
    grad_middle = grad_out + norm_back(grad_hidden_two, normed_two, inverse_two, gain_two)
    grad_branch = grad_middle.astype(LOW)
    grad_mixed_own = right_dot(grad_branch, out_full).astype(LOW)
    grad_mixed_sent = grad_mixed_own.reshape(rows, GROUP, shard).transpose(1, 0, 2)
    grad_mixed = links.exchange(grad_mixed_sent)
    grad_mixed = grad_mixed.reshape(GROUP * rows, shard)

    feed_half = links.core_sum(feed_near, feed_far, order_zero(grad_mixed_sent))
    block_out = links.chip_sum(feed_half.reshape(4, rows, width))
    block_out = (middle + block_out + bias_down).astype(LOW)

    pieces = [left_dot(hidden_two, grad_pre_low).astype(LOW).reshape(planes, -1, hidden_shard)]
    for start in range(0, width, hidden_shard):
        piece = left_dot(activated_low, grad_feed[:, start : start + hidden_shard]).astype(LOW)
        pieces.append(piece.reshape(planes, own_hidden, hidden_shard))
    both_rows = lax.psum_scatter(
        jnp.concatenate(pieces, axis=1), "dp", axis_index_groups=links.plane_groups()
    )
    up_rows = both_rows[: GROUP * own_rows].reshape(GROUP, own_rows, hidden_shard)
    grad_down_w = both_rows[GROUP * own_rows :].reshape(-1, own_hidden, hidden_shard)
    grad_down_w = grad_down_w.transpose(1, 0, 2).reshape(own_hidden, width).astype(WIDE)

    grad_packed, near, far, norm_sums, packed_sums = attention_back(
        packed, grad_mixed, allowed, qkv_full, normed_low, places, block_out
    )
    proj_rows = left_dot(hidden_one, grad_packed).astype(LOW)
    proj_rows = proj_rows.reshape(planes, GROUP, own_rows, heads_width)
    proj_sum = links.plane_sum(proj_rows)
    grad_hidden_half = links.core_sum(near, far)
    grad_hidden_one = links.chip_exchange(grad_hidden_half)
    out_parts = left_dot(mixed, grad_branch).astype(LOW)
    out_parts = out_parts.reshape(planes, GROUP, own_rows, width)
    out_near, out_far = (
        jnp.stack(
            [lax.dynamic_index_in_dim(out_parts, place ^ r, 1, False) for r in order]
        ).reshape(4, planes * own_rows, width)
        for order in ((0, 2, 4, 6), (1, 3, 5, 7))
    )
    out_half = links.core_sum(out_near, out_far, order_zero(proj_sum))
    out_sum = links.chip_sum(out_half).astype(LOW)

    normed_one, inverse_one = norm_rows(token_rows)
    grad_inputs = grad_middle + norm_back(grad_hidden_one, normed_one, inverse_one, gain_one)

    proj_sums = jnp.zeros((2, width), WIDE)
    proj_sums = lax.dynamic_update_slice_in_dim(
        proj_sums,
        jnp.concatenate([packed_sums[:, :shard], packed_sums[:, 2 * shard :]], axis=0),
        place * shard,
        1,
    )
    up_sums = jnp.zeros((planes, GROUP, own_hidden), WIDE)
    up_sums = lax.dynamic_update_index_in_dim(
        up_sums, up_bias_sums.reshape(planes, own_hidden), place, 1
    )
    vectors = [
        norm_sums[0],
        norm_sums[1],
        jnp.sum(grad_branch.astype(WIDE), axis=0),
        jnp.sum(grad_hidden_two * normed_two, axis=0),
        jnp.sum(grad_hidden_two, axis=0),
        jnp.sum(grad_feed_own.astype(WIDE), axis=0),
        proj_sums,
        up_sums,
    ]
    vectors = jnp.concatenate([v.reshape(planes, GROUP, -1) for v in vectors], axis=2)
    grad_out_w = links.plane_sum(out_sum.reshape(planes, own_rows, width))
    vectors = vectors.reshape(count, -1) + order_zero(grad_hidden_one)
    sums = jnp.sum(lax.all_to_all(vectors, "dp", 0, 0, tiled=True), axis=0)
    proj_rows = (proj_sum + order_zero(sums)).astype(LOW)
    row_blocks = links.exchange(jnp.concatenate([proj_rows, up_rows], axis=2))
    row_blocks = row_blocks.astype(WIDE)
    grad_proj_w = row_blocks[:, :, :heads_width]
    grad_proj_w = grad_proj_w.reshape(GROUP, own_rows, 3, shard).transpose(1, 2, 0, 3)
    grad_proj_w = grad_proj_w.reshape(own_rows, 3 * width)
    grad_up_w = row_blocks[:, :, heads_width:]
    grad_up_w = grad_up_w.reshape(GROUP, own_rows, planes, own_hidden).transpose(1, 2, 0, 3)
    grad_up_w = grad_up_w.reshape(own_rows, hidden)

    grads = [sums[i * own_rows : (i + 1) * own_rows] for i in range(6)]
    grad_proj_b = sums[6 * own_rows : 8 * own_rows]
    grad_up_b = sums[8 * own_rows :]
    return (
        block_out,
        grad_inputs,
        grads[0],
        grads[1],
        grad_proj_w,
        grad_proj_b,
        grad_out_w,
        grads[2],
        grads[3],
        grads[4],
        grad_up_w,
        grad_up_b,
        grad_down_w,
        grads[5],
    )


def solution(mesh):
    flat, wide = P("dp"), P("dp", None)
    in_specs = (
        (wide, flat, flat, flat, flat, wide, flat, wide, flat, flat, flat, wide, flat, wide)
        + (flat, wide)
    )
    out_specs = (
        (wide, wide, flat, flat, wide, flat, wide, flat, flat, flat, wide, flat, wide, flat)
    )
    return jax.shard_map(local, mesh=mesh, in_specs=in_specs, out_specs=out_specs, check_vma=False)
```

```python
import functools
import math

import jax
import jax.numpy as jnp
from jax import lax
from jax.experimental import pallas as pl
from jax.experimental.pallas import tpu as pltpu
from jax.sharding import PartitionSpec as P

HEAD_DIM = 64
EPS = 1e-05
NEG = -1e30
GROUP = 8
DIRECT_PLANES = 8
VMEM_BYTES = 56 << 20
LOW = jnp.bfloat16
WIDE = jnp.float32


def norm_rows(inputs):
    average = jnp.mean(inputs, axis=-1, keepdims=True)
    centered = inputs - average
    variance = jnp.mean(centered * centered, axis=-1, keepdims=True)
    inverse = lax.rsqrt(variance + EPS)
    return (centered * inverse, inverse)


def norm_back(grad_in, normed, inverse, gain):
    scaled = grad_in * gain
    return inverse * (
        scaled
        - jnp.mean(scaled, axis=1, keepdims=True)
        - normed * jnp.mean(scaled * normed, axis=1, keepdims=True)
    )


def gelu_tanh(inputs):
    return (
        0.5
        * inputs
        * (1.0 + jnp.tanh(0.7978845608028654 * (inputs + 0.044715 * inputs * inputs * inputs)))
    )


def dot(first, second, dims):
    return lax.dot_general(first, second, (dims, ((), ())), preferred_element_type=jnp.float32)


def plain_dot(first, second):
    return dot(first, second, ((1,), (0,)))


def left_dot(first, second):
    return dot(first, second, ((0,), (0,)))


def right_dot(first, second):
    return dot(first, second, ((1,), (1,)))


def head_masks():
    lane = lax.broadcasted_iota(jnp.int32, (1, 2 * HEAD_DIM), 1)
    return [((lane // HEAD_DIM) == h).astype(LOW) for h in range(2)]


def softmax_rows(query, key, allowed):
    scores = right_dot(query, key) * (1.0 / math.sqrt(HEAD_DIM))
    scores = jnp.where(allowed, scores, NEG)
    top = jnp.max(scores, axis=1, keepdims=True)
    raw = jnp.exp(scores - top)
    return raw / jnp.sum(raw, axis=1, keepdims=True)


def pick_block(step, refs, target_ref):
    for k, ref in enumerate(refs):

        @pl.when(step == k)
        def _(ref=ref):
            target_ref[...] = ref[...]


def attention_kernel(place_ref, *refs):
    token_refs, refs = refs[:GROUP], refs[GROUP:]
    gain_ref, offset_ref, bias_ref, pieces_ref, allowed_ref, *refs = refs
    hidden_ref, normed_ref, packed_ref, weight_ref, out_ref, block_ref = refs
    step = pl.program_id(0)
    width = 2 * HEAD_DIM
    own_rows = weight_ref.shape[0] // pieces_ref.shape[0]

    @pl.when(step == 0)
    def _():
        for part in range(3):
            piece = pieces_ref[:, part * own_rows : (part + 1) * own_rows, :]
            weight_ref[:, part * width : (part + 1) * width] = piece.reshape(-1, width)

    pick_block(step, token_refs, block_ref)
    normed, _ = norm_rows(block_ref[...].astype(WIDE))
    hidden = (normed * gain_ref[...] + offset_ref[...]).astype(LOW)
    normed_ref[...] = normed.astype(LOW)
    hidden_ref[...] = hidden
    packed = (plain_dot(hidden, weight_ref[...]) + bias_ref[...]).astype(LOW)
    packed_ref[...] = packed
    key, value = packed[:, width : 2 * width], packed[:, 2 * width :]
    allowed = allowed_ref[0] > 0
    total = None
    for mask in head_masks():
        weights = softmax_rows(packed[:, :width] * mask, key, allowed).astype(LOW)
        term = plain_dot(weights, value * mask)
        total = term if total is None else total + term
    out_ref[...] = total.astype(LOW)


def attention_back_kernel(
    packed_ref,
    grad_ref,
    allowed_ref,
    weight_ref,
    normed_ref,
    out_ref,
    near_ref,
    far_ref,
    norm_sums_ref,
    bias_sums_ref,
):
    masks = head_masks()
    rows = allowed_ref.shape[1]
    width = 2 * HEAD_DIM
    scale = 1.0 / math.sqrt(HEAD_DIM)
    for block in range(allowed_ref.shape[0]):
        part = pl.ds(block * rows, rows)
        query = packed_ref[part, :width]
        key = packed_ref[part, width : 2 * width]
        value = packed_ref[part, 2 * width :]
        grad = grad_ref[part, :]
        allowed = allowed_ref[block] > 0
        sums = [None, None, None]
        for mask in masks:
            query_head = query * mask
            grad_head = grad * mask
            weights = softmax_rows(query_head, key, allowed)
            grad_weights = right_dot(grad_head, value)
            grad_scores = weights * (
                grad_weights - jnp.sum(grad_weights * weights, axis=1, keepdims=True)
            )
            grad_scores = grad_scores.astype(LOW)
            terms = (
                plain_dot(grad_scores, key * mask),
                left_dot(grad_scores, query_head),
                left_dot(weights.astype(LOW), grad_head),
            )
            sums = [t if s is None else s + t for s, t in zip(sums, terms)]
        out_ref[part, :width] = (sums[0] * scale).astype(LOW)
        out_ref[part, width : 2 * width] = (sums[1] * scale).astype(LOW)
        out_ref[part, 2 * width :] = sums[2].astype(LOW)
    grad_hidden = right_dot(out_ref[...], weight_ref[...])
    hidden = grad_hidden.astype(LOW)
    step = pl.program_id(0)
    gain_sums = jnp.sum(grad_hidden * normed_ref[...].astype(WIDE), axis=0, keepdims=True)
    plain_sums = jnp.sum(grad_hidden, axis=0, keepdims=True)
    norm_sums = jnp.concatenate([gain_sums, plain_sums], axis=0)
    bias_sums = jnp.sum(out_ref[...].astype(WIDE), axis=0, keepdims=True)

    @pl.when(step == 0)
    def _():
        norm_sums_ref[...] = norm_sums
        bias_sums_ref[...] = bias_sums

    @pl.when(step > 0)
    def _():
        norm_sums_ref[...] += norm_sums
        bias_sums_ref[...] += bias_sums

    @pl.when(step < pl.num_programs(0) // 2)
    def _():
        near_ref[...] = hidden

    @pl.when(step >= pl.num_programs(0) // 2)
    def _():
        far_ref[...] = hidden


def block_place(i, place_ref):
    return place_ref[0] ^ (((i & 3) << 1) | (i >> 2))


def fixed(shape):
    return pl.BlockSpec(shape, lambda i, p: (0,) * len(shape))


def attention(blocks, gain, offset, bias, pieces, allowed, places):
    rows, model_width = blocks[0].shape
    width = 2 * HEAD_DIM
    count = len(blocks)
    return pl.pallas_call(
        attention_kernel,
        grid_spec=pltpu.PrefetchScalarGridSpec(
            num_scalar_prefetch=1,
            grid=(count,),
            in_specs=[fixed((rows, model_width))] * count
            + [
                fixed((1, model_width)),
                fixed((1, model_width)),
                fixed((1, 3 * width)),
                fixed(pieces.shape),
                pl.BlockSpec((1, rows, rows), lambda i, p: (block_place(i, p), 0, 0)),
            ],
            out_specs=[
                pl.BlockSpec((rows, model_width), lambda i, p: (i, 0)),
                pl.BlockSpec((rows, model_width), lambda i, p: (i, 0)),
                pl.BlockSpec((rows, 3 * width), lambda i, p: (i, 0)),
                fixed((model_width, 3 * width)),
                pl.BlockSpec((rows, width), lambda i, p: (block_place(i, p), 0)),
            ],
            scratch_shapes=[pltpu.VMEM((rows, model_width), LOW)],
        ),
        out_shape=[
            jax.ShapeDtypeStruct((count * rows, model_width), LOW),
            jax.ShapeDtypeStruct((count * rows, model_width), LOW),
            jax.ShapeDtypeStruct((count * rows, 3 * width), LOW),
            jax.ShapeDtypeStruct((model_width, 3 * width), LOW),
            jax.ShapeDtypeStruct((count * rows, width), LOW),
        ],
        compiler_params=pltpu.CompilerParams(vmem_limit_bytes=VMEM_BYTES),
        cost_estimate=pl.CostEstimate(
            flops=8 * count * rows * rows * width,
            bytes_accessed=count * rows * model_width,
            transcendentals=0,
        ),
    )(places, *blocks, gain, offset, bias, pieces, allowed)


def attention_back(packed, grad, allowed, weight, normed, places, earlier):
    blocks, rows, _ = allowed.shape
    width = 2 * HEAD_DIM
    model_width = weight.shape[0]
    half = blocks // 2
    return pl.pallas_call(
        lambda place_ref, a_ref, *refs: attention_back_kernel(*refs),
        grid_spec=pltpu.PrefetchScalarGridSpec(
            num_scalar_prefetch=1,
            grid=(blocks,),
            in_specs=[
                pl.BlockSpec(memory_space=pl.ANY),
                pl.BlockSpec((rows, 3 * width), lambda i, p: (i, 0)),
                pl.BlockSpec((rows, width), lambda i, p: (block_place(i, p), 0)),
                pl.BlockSpec((1, rows, rows), lambda i, p: (block_place(i, p), 0, 0)),
                pl.BlockSpec((model_width, 3 * width), lambda i, p: (0, 0)),
                pl.BlockSpec((rows, model_width), lambda i, p: (i, 0)),
            ],
            out_specs=[
                pl.BlockSpec((rows, 3 * width), lambda i, p: (i, 0)),
                pl.BlockSpec(
                    (rows, model_width), lambda i, p: ((p[0] >> 1) ^ jnp.minimum(i, half - 1), 0)
                ),
                pl.BlockSpec(
                    (rows, model_width),
                    lambda i, p: ((p[0] >> 1) ^ (jnp.maximum(i, half) - half), 0),
                ),
                pl.BlockSpec((2, model_width), lambda i, p: (0, 0)),
                pl.BlockSpec((1, 3 * width), lambda i, p: (0, 0)),
            ],
        ),
        out_shape=[
            jax.ShapeDtypeStruct((blocks * rows, 3 * width), LOW),
            jax.ShapeDtypeStruct((half * rows, model_width), LOW),
            jax.ShapeDtypeStruct((half * rows, model_width), LOW),
            jax.ShapeDtypeStruct((2, model_width), WIDE),
            jax.ShapeDtypeStruct((1, 3 * width), WIDE),
        ],
        compiler_params=pltpu.CompilerParams(vmem_limit_bytes=VMEM_BYTES),
        cost_estimate=pl.CostEstimate(
            flops=20 * blocks * rows * rows * width,
            bytes_accessed=4 * packed.size + 4 * allowed.size,
            transcendentals=2 * allowed.size,
        ),
    )(places, earlier, packed, grad, allowed, weight, normed)


def feed_kernel(place_ref, *refs):
    input_refs, grad_refs, refs = refs[:GROUP], refs[GROUP : 2 * GROUP], refs[2 * GROUP :]
    planes = len(refs) - 11
    up_refs, refs = refs[:planes], refs[planes:]
    down_ref, bias_ref, input_ref, grad_ref, act_ref, pre_ref, sums_ref, near_ref, far_ref = refs[:9]
    up_ref = refs[9]
    step = pl.program_id(0)
    rows = input_ref.shape[0] // 2
    pick_block(step, input_refs[0::2], input_ref.at[pl.ds(0, rows)])
    pick_block(step, input_refs[1::2], input_ref.at[pl.ds(rows, rows)])
    pick_block(step, grad_refs[0::2], grad_ref.at[pl.ds(0, rows)])
    pick_block(step, grad_refs[1::2], grad_ref.at[pl.ds(rows, rows)])

    @pl.when(step == 0)
    def _():
        for k, ref in enumerate(up_refs):
            depth = ref.shape[0] * ref.shape[1]
            source = lax.rem(place_ref[1] + planes - k, planes) * depth
            up_ref[pl.ds(pl.multiple_of(source, depth), depth), :] = ref[...].reshape(depth, -1)

    root, cube = 0.7978845608028654, 0.044715
    pre = plain_dot(input_ref[...], up_ref[...]) + bias_ref[...]
    square = pre * pre
    bend = jnp.tanh(root * (pre + cube * square * pre))
    act_ref[...] = (0.5 * pre * (1.0 + bend)).astype(LOW)
    slope = 0.5 * (1.0 + bend) + 0.5 * pre * (1.0 - bend * bend) * (
        root * (1.0 + 3.0 * cube * square)
    )
    grad_pre = (right_dot(grad_ref[...], down_ref[...]) * slope).astype(LOW)
    pre_ref[...] = grad_pre
    sums = jnp.sum(grad_pre.astype(WIDE), axis=0, keepdims=True)

    @pl.when(step == 0)
    def _():
        sums_ref[...] = sums

    @pl.when(step > 0)
    def _():
        sums_ref[...] += sums

    hidden = right_dot(grad_pre, up_ref[...]).astype(LOW)
    odd = (place_ref[0] >> 1) & 1
    first = pl.ds(pl.multiple_of(odd * rows, rows), rows)
    second = pl.ds(pl.multiple_of((1 - odd) * rows, rows), rows)
    for ref, wanted in (
        (near_ref, step < pl.num_programs(0) // 2),
        (far_ref, step >= pl.num_programs(0) // 2),
    ):

        @pl.when(wanted)
        def _(ref=ref):
            ref[first, :] = hidden[:rows]
            ref[second, :] = hidden[rows:]


def feed_forward(inputs, grads, up_parts, down, bias, places):
    block_rows, width = inputs[0].shape
    hidden = down.shape[0]
    tokens = GROUP * block_rows
    rows = 2 * block_rows
    steps = tokens // rows
    half = steps // 2
    return pl.pallas_call(
        feed_kernel,
        grid_spec=pltpu.PrefetchScalarGridSpec(
            num_scalar_prefetch=1,
            grid=(steps,),
            in_specs=[fixed((block_rows, width))] * (2 * GROUP)
            + [fixed(part.shape) for part in up_parts]
            + [fixed((hidden, width)), fixed((1, hidden))],
            out_specs=[
                pl.BlockSpec((rows, width), lambda i, p: (i, 0)),
                pl.BlockSpec((rows, width), lambda i, p: (i, 0)),
                pl.BlockSpec((rows, hidden), lambda i, p: (i, 0)),
                pl.BlockSpec((rows, hidden), lambda i, p: (i, 0)),
                fixed((1, hidden)),
                pl.BlockSpec((rows, width), lambda i, p: ((p[0] >> 2) ^ jnp.minimum(i, half - 1), 0)),
                pl.BlockSpec(
                    (rows, width), lambda i, p: ((p[0] >> 2) ^ (jnp.maximum(i, half) - half), 0)
                ),
            ],
            scratch_shapes=[pltpu.VMEM((width, hidden), LOW), pltpu.SMEM((1,), jnp.int32)],
        ),
        out_shape=[
            jax.ShapeDtypeStruct((tokens, width), LOW),
            jax.ShapeDtypeStruct((tokens, width), LOW),
            jax.ShapeDtypeStruct((tokens, hidden), LOW),
            jax.ShapeDtypeStruct((tokens, hidden), LOW),
            jax.ShapeDtypeStruct((1, hidden), WIDE),
            jax.ShapeDtypeStruct((tokens // 2, width), LOW),
            jax.ShapeDtypeStruct((tokens // 2, width), LOW),
        ],
        compiler_params=pltpu.CompilerParams(vmem_limit_bytes=VMEM_BYTES),
        cost_estimate=pl.CostEstimate(
            flops=tokens * width * hidden,
            bytes_accessed=tokens * width,
            transcendentals=0,
        ),
    )(places, *inputs, *grads, *up_parts, down, bias)


def branch_kernel(place_ref, earlier_ref, act_ref, down_ref, out_ref):
    rows = act_ref.shape[0] // 2
    result = plain_dot(act_ref[...], down_ref[...]).astype(LOW)
    odd = (place_ref[0] >> 1) & 1
    out_ref[pl.ds(pl.multiple_of(odd * rows, rows), rows), :] = result[:rows]
    out_ref[pl.ds(pl.multiple_of((1 - odd) * rows, rows), rows), :] = result[rows:]


def branch_terms(act, down, places, earlier):
    tokens, hidden = act.shape
    width = down.shape[1]
    rows = 2 * tokens // GROUP
    return pl.pallas_call(
        branch_kernel,
        grid_spec=pltpu.PrefetchScalarGridSpec(
            num_scalar_prefetch=1,
            grid=(tokens // rows,),
            in_specs=[
                pl.BlockSpec(memory_space=pl.ANY),
                pl.BlockSpec((rows, hidden), lambda i, p: (i, 0)),
                fixed((hidden, width)),
            ],
            out_specs=pl.BlockSpec(
                (rows, width),
                lambda i, p: (2 * ((p[0] & 1) ^ (i >> 1)) + ((p[0] >> 2) ^ (i & 1)), 0),
            ),
        ),
        out_shape=jax.ShapeDtypeStruct((tokens, width), LOW),
        compiler_params=pltpu.CompilerParams(vmem_limit_bytes=VMEM_BYTES),
    )(places, earlier, act, down)


class Links:
    def __init__(self, count):
        self.count = count
        self.planes = count // GROUP
        index = lax.axis_index("dp")
        self.place = index & (GROUP - 1)
        self.plane = index // GROUP

    def swap(self, array, flip):
        return lax.ppermute(array, "dp", [(i, i ^ flip) for i in range(self.count)])

    def shift(self, array, steps):
        hop = steps * GROUP
        return lax.ppermute(array, "dp", [(i, (i + hop) % self.count) for i in range(self.count)])

    def group_gather(self, block):
        near = [block] + [None] * 3
        for k in (3, 1, 2):
            near[k] = self.swap(block, 2 * k)
        far = [self.swap(b, 1) for b in near]
        return near + far

    def core_sum(self, near, far, order=0.0):
        return (near.astype(WIDE) + (self.swap(far, 1).astype(WIDE) + order)).astype(LOW)

    def chip_sum(self, halves):
        total = halves[0].astype(WIDE)
        for k in (3, 1, 2):
            total = total + self.swap(halves[k], 2 * k).astype(WIDE)
        return total

    def chip_exchange(self, halves):
        chips = GROUP // 2
        groups = [
            [p * GROUP + 2 * m + c for m in range(chips)]
            for p in range(self.planes)
            for c in range(2)
        ]
        parts = halves.reshape(chips, halves.shape[0] // chips, halves.shape[1])
        terms = lax.all_to_all(parts, "dp", 0, 0, axis_index_groups=groups, tiled=True)
        return jnp.sum(terms.astype(WIDE), axis=0)

    def core_lists(self):
        order = [2 * m + c for c in range(2) for m in range(GROUP // 2)]
        return [[p * GROUP + j for j in order] for p in range(self.planes)]

    def group_lists(self):
        return [[p * GROUP + j for j in range(GROUP)] for p in range(self.planes)]

    def plane_exchange(self, parts):
        return lax.all_to_all(
            parts, "dp", 0, 0, axis_index_groups=self.plane_groups(), tiled=True
        )

    def exchange(self, parts):
        return lax.all_to_all(
            parts, "dp", 0, 0, axis_index_groups=self.group_lists(), tiled=True
        )

    def plane_groups(self):
        return [[p * GROUP + j for p in range(self.planes)] for j in range(GROUP)]

    def plane_gather(self, block):
        if self.planes > DIRECT_PLANES:
            found = lax.all_gather(block, "dp", axis_index_groups=self.plane_groups())
            return [
                lax.dynamic_index_in_dim(found, (self.plane - k) % self.planes, 0, False)
                for k in range(self.planes)
            ]
        return [block] + [self.shift(block, k) for k in range(1, self.planes)]

    def plane_sum(self, chunks):
        if self.planes > DIRECT_PLANES:
            return lax.psum_scatter(
                chunks.astype(WIDE), "dp", axis_index_groups=self.plane_groups()
            )
        total = lax.dynamic_index_in_dim(chunks, self.plane, 0, False).astype(WIDE)
        for k in range(1, self.planes):
            target = (self.plane + k) % self.planes
            term = lax.dynamic_index_in_dim(chunks, target, 0, False)
            total = total + self.shift(term, k).astype(WIDE)
        return total


def order_zero(array):
    return array[(0,) * array.ndim].astype(WIDE) * 0.0


def local(
    tokens,
    segment_ids,
    pad_mask,
    ln1_gain,
    ln1_bias,
    qkv_weight,
    qkv_bias,
    out_weight,
    out_bias,
    ln2_gain,
    ln2_bias,
    up_weight,
    up_bias,
    down_weight,
    down_bias,
    cotangent,
):
    count = lax.axis_size("dp")
    links = Links(count)
    place, planes = links.place, links.planes
    rows, width = tokens.shape
    own_rows = qkv_weight.shape[0]
    hidden = up_weight.shape[1]
    shard = width // GROUP
    hidden_shard = hidden // GROUP
    own_hidden = hidden // count
    heads_width = 3 * shard

    code = (segment_ids * 2 + pad_mask).astype(LOW)
    fill = jnp.zeros((shard - 4 * own_rows,), LOW)
    wide_fill = jnp.zeros((shard - own_hidden,), LOW)
    empty = jnp.zeros((shard,), LOW)
    small = [
        jnp.concatenate([ln1_gain, ln1_bias, out_bias, ln2_gain, fill]),
        jnp.concatenate([ln2_bias, down_bias, qkv_bias, fill]),
        jnp.concatenate([up_bias, wide_fill]),
        code,
    ]
    small = jnp.stack(small + [empty] * 4)
    qkv_parts = qkv_weight.reshape(own_rows, 3, GROUP, shard).transpose(2, 1, 0, 3)
    qkv_parts = qkv_parts.reshape(GROUP, 3 * own_rows, shard)
    small_parts = jnp.broadcast_to(small[None], (GROUP,) + small.shape)
    sent = jnp.concatenate([qkv_parts, small_parts], axis=1)
    sent = jnp.broadcast_to(sent[None], (planes,) + sent.shape).reshape((count,) + sent.shape[1:])
    up_parts = up_weight.reshape(own_rows, planes, GROUP, own_hidden)
    up_parts = up_parts.transpose(2, 0, 1, 3).reshape(GROUP, own_rows, hidden_shard)
    up_plane = links.exchange(up_parts)
    sent = sent + order_zero(up_plane).astype(LOW)
    token_blocks = links.group_gather(tokens)
    grad_out = cotangent.astype(WIDE) * pad_mask.astype(WIDE)[:, None]
    grad_feed_own = grad_out.astype(LOW)
    grad_feed_blocks = links.group_gather(grad_feed_own)
    buffer = lax.all_to_all(sent, "dp", 0, 0, tiled=True)
    out_full = lax.all_gather(out_weight, "dp", axis=0, tiled=True)
    down_full = lax.all_gather(
        down_weight, "dp", axis_index_groups=links.plane_groups(), tiled=True
    )
    def small_vector(row, start, length):
        start = start * own_rows
        return buffer[:, 3 * own_rows + row, start : start + length].astype(WIDE)

    gain_one, bias_one, bias_out, gain_two, bias_two, bias_down = (
        small_vector(i // 4, i % 4, own_rows).reshape(width) for i in range(6)
    )
    qkv_bias_all = small_vector(1, 2, 2 * own_rows).reshape(2, width)
    bias_qv = lax.dynamic_slice_in_dim(qkv_bias_all, place * shard, shard, 1)
    bias_heads = jnp.concatenate([bias_qv[0], jnp.zeros((shard,), WIDE), bias_qv[1]])
    up_bias_all = small_vector(2, 0, own_hidden).reshape(planes, GROUP, own_hidden)
    bias_up = lax.dynamic_index_in_dim(up_bias_all, place, 1, False).reshape(hidden_shard)

    codes = lax.dynamic_slice_in_dim(small_vector(3, 0, rows), links.plane * GROUP, GROUP, 0)
    codes = codes.astype(jnp.int32)
    segments, live = codes >> 1, codes & 1
    positions = jnp.arange(rows, dtype=jnp.int32)
    allowed = (
        (segments[:, :, None] == segments[:, None, :])
        & (positions[None, :] <= positions[:, None])[None]
        & (live[:, None, :] == 1)
    ).astype(WIDE)

    places = jnp.stack([place, links.plane])
    hidden_one, normed_low, packed, qkv_full, mixed_heads = attention(
        token_blocks,
        gain_one[None],
        bias_one[None],
        bias_heads[None],
        buffer,
        allowed,
        places,
    )
    up_blocks = links.plane_gather(up_plane)
    mixed_heads = mixed_heads.reshape(GROUP, rows, shard)
    mixed = links.exchange(mixed_heads)
    mixed = mixed.transpose(1, 0, 2).reshape(rows, width)
    token_rows = tokens.astype(WIDE)
    middle = token_rows + (plain_dot(mixed, out_full) + bias_out)
    normed_two, inverse_two = norm_rows(middle)
    hidden_two_own = (normed_two * gain_two + bias_two).astype(LOW)
    up_here = sum(order_zero(b) for b in up_blocks[1:])
    hidden_two_own = (hidden_two_own.astype(WIDE) + up_here).astype(LOW)
    hidden_two_blocks = links.group_gather(hidden_two_own)

    half_rows = GROUP * rows // 2
    hidden_two, grad_feed, activated_low, grad_pre_low, up_bias_sums, near, far = feed_forward(
        hidden_two_blocks, grad_feed_blocks, up_blocks, down_full, bias_up[None], places
    )
    grad_hidden_half = links.core_sum(near, far)
    grad_hidden_two = links.chip_exchange(grad_hidden_half)
    grad_middle = grad_out + norm_back(grad_hidden_two, normed_two, inverse_two, gain_two)
    grad_branch = grad_middle.astype(LOW)
    grad_mixed_own = right_dot(grad_branch, out_full).astype(LOW)
    grad_mixed_sent = grad_mixed_own.reshape(rows, GROUP, shard).transpose(1, 0, 2)
    grad_mixed = links.exchange(grad_mixed_sent)
    grad_mixed = grad_mixed.reshape(GROUP * rows, shard)

    out_parts = left_dot(mixed, grad_branch).astype(LOW)
    out_parts = out_parts.reshape(planes, GROUP, own_rows, width)
    out_near, out_far = (
        jnp.stack(
            [lax.dynamic_index_in_dim(out_parts, place ^ r, 1, False) for r in order]
        ).reshape(4, planes * own_rows, width)
        for order in ((0, 2, 4, 6), (1, 3, 5, 7))
    )
    out_half = links.core_sum(out_near, out_far)

    pieces = [left_dot(hidden_two, grad_pre_low).astype(LOW).reshape(planes, -1, hidden_shard)]
    for start in range(0, width, hidden_shard):
        piece = left_dot(activated_low, grad_feed[:, start : start + hidden_shard]).astype(LOW)
        pieces.append(piece.reshape(planes, own_hidden, hidden_shard))
    both_rows = lax.psum_scatter(
        jnp.concatenate(pieces, axis=1), "dp", axis_index_groups=links.plane_groups()
    )
    up_rows = both_rows[: GROUP * own_rows].reshape(GROUP, own_rows, hidden_shard)
    grad_down_w = both_rows[GROUP * own_rows :].reshape(-1, own_hidden, hidden_shard)
    grad_down_w = grad_down_w.transpose(1, 0, 2).reshape(own_hidden, width).astype(WIDE)

    grad_packed, near, far, norm_sums, packed_sums = attention_back(
        packed, grad_mixed, allowed, qkv_full, normed_low, places, out_half
    )
    proj_rows = left_dot(hidden_one, grad_packed).astype(LOW)
    proj_rows = proj_rows.reshape(planes, GROUP, own_rows, heads_width)
    proj_sum = links.plane_sum(proj_rows)
    grad_hidden_half = links.core_sum(near, far)
    grad_hidden_one = links.chip_exchange(grad_hidden_half)
    feed_parts = branch_terms(activated_low, down_full, places, grad_hidden_half)
    feed = lax.psum_scatter(
        feed_parts, "dp", axis_index_groups=links.core_lists(), scatter_dimension=0, tiled=True
    )
    block_out = (middle + feed.astype(WIDE) + bias_down).astype(LOW)
    out_chips = (out_half + order_zero(grad_hidden_one).astype(LOW)).reshape(4, -1, width)
    out_sum = links.chip_sum(out_chips).astype(LOW)
    normed_one, inverse_one = norm_rows(token_rows)
    grad_inputs = grad_middle + norm_back(grad_hidden_one, normed_one, inverse_one, gain_one)

    proj_sums = jnp.zeros((2, width), WIDE)
    proj_sums = lax.dynamic_update_slice_in_dim(
        proj_sums,
        jnp.concatenate([packed_sums[:, :shard], packed_sums[:, 2 * shard :]], axis=0),
        place * shard,
        1,
    )
    up_sums = jnp.zeros((planes, GROUP, own_hidden), WIDE)
    up_sums = lax.dynamic_update_index_in_dim(
        up_sums, up_bias_sums.reshape(planes, own_hidden), place, 1
    )
    vectors = [
        norm_sums[0],
        norm_sums[1],
        jnp.sum(grad_branch.astype(WIDE), axis=0),
        jnp.sum(grad_hidden_two * normed_two, axis=0),
        jnp.sum(grad_hidden_two, axis=0),
        jnp.sum(grad_feed_own.astype(WIDE), axis=0),
        proj_sums,
        up_sums,
    ]
    vectors = jnp.concatenate([v.reshape(planes, GROUP, -1) for v in vectors], axis=2)
    grad_out_w = links.plane_sum(out_sum.reshape(planes, own_rows, width))
    vectors = vectors.reshape(count, -1) + order_zero(grad_hidden_one)
    sums = jnp.sum(lax.all_to_all(vectors, "dp", 0, 0, tiled=True), axis=0)
    proj_rows = (proj_sum + order_zero(sums)).astype(LOW)
    row_blocks = links.exchange(jnp.concatenate([proj_rows, up_rows], axis=2))
    row_blocks = row_blocks.astype(WIDE)
    grad_proj_w = row_blocks[:, :, :heads_width]
    grad_proj_w = grad_proj_w.reshape(GROUP, own_rows, 3, shard).transpose(1, 2, 0, 3)
    grad_proj_w = grad_proj_w.reshape(own_rows, 3 * width)
    grad_up_w = row_blocks[:, :, heads_width:]
    grad_up_w = grad_up_w.reshape(GROUP, own_rows, planes, own_hidden).transpose(1, 2, 0, 3)
    grad_up_w = grad_up_w.reshape(own_rows, hidden)

    grads = [sums[i * own_rows : (i + 1) * own_rows] for i in range(6)]
    grad_proj_b = sums[6 * own_rows : 8 * own_rows]
    grad_up_b = sums[8 * own_rows :]
    return (
        block_out,
        grad_inputs,
        grads[0],
        grads[1],
        grad_proj_w,
        grad_proj_b,
        grad_out_w,
        grads[2],
        grads[3],
        grads[4],
        grad_up_w,
        grad_up_b,
        grad_down_w,
        grads[5],
    )


def solution(mesh):
    flat, wide = P("dp"), P("dp", None)
    in_specs = (
        (wide, flat, flat, flat, flat, wide, flat, wide, flat, flat, flat, wide, flat, wide)
        + (flat, wide)
    )
    out_specs = (
        (wide, wide, flat, flat, wide, flat, wide, flat, flat, flat, wide, flat, wide, flat)
    )
    return jax.shard_map(local, mesh=mesh, in_specs=in_specs, out_specs=out_specs, check_vma=False)
```

```python
import functools
import math

import jax
import jax.numpy as jnp
from jax import lax
from jax.experimental import pallas as pl
from jax.experimental.pallas import tpu as pltpu
from jax.sharding import PartitionSpec as P

HEAD_DIM = 64
EPS = 1e-05
NEG = -1e30
GROUP = 8
DIRECT_PLANES = 8
VMEM_BYTES = 56 << 20
LOW = jnp.bfloat16
WIDE = jnp.float32


def norm_rows(inputs):
    average = jnp.mean(inputs, axis=-1, keepdims=True)
    centered = inputs - average
    variance = jnp.mean(centered * centered, axis=-1, keepdims=True)
    inverse = lax.rsqrt(variance + EPS)
    return (centered * inverse, inverse)


def norm_back(grad_in, normed, inverse, gain):
    scaled = grad_in * gain
    return inverse * (
        scaled
        - jnp.mean(scaled, axis=1, keepdims=True)
        - normed * jnp.mean(scaled * normed, axis=1, keepdims=True)
    )


def gelu_tanh(inputs):
    return (
        0.5
        * inputs
        * (1.0 + jnp.tanh(0.7978845608028654 * (inputs + 0.044715 * inputs * inputs * inputs)))
    )


def dot(first, second, dims):
    return lax.dot_general(first, second, (dims, ((), ())), preferred_element_type=jnp.float32)


def plain_dot(first, second):
    return dot(first, second, ((1,), (0,)))


def left_dot(first, second):
    return dot(first, second, ((0,), (0,)))


def right_dot(first, second):
    return dot(first, second, ((1,), (1,)))


def head_masks():
    lane = lax.broadcasted_iota(jnp.int32, (1, 2 * HEAD_DIM), 1)
    return [((lane // HEAD_DIM) == h).astype(LOW) for h in range(2)]


def softmax_rows(query, key, allowed):
    scores = right_dot(query, key) * (1.0 / math.sqrt(HEAD_DIM))
    scores = jnp.where(allowed, scores, NEG)
    top = jnp.max(scores, axis=1, keepdims=True)
    raw = jnp.exp(scores - top)
    return raw / jnp.sum(raw, axis=1, keepdims=True)


def pick_block(step, refs, target_ref):
    for k, ref in enumerate(refs):

        @pl.when(step == k)
        def _(ref=ref):
            target_ref[...] = ref[...]


def attention_kernel(place_ref, *refs):
    token_refs, refs = refs[:GROUP], refs[GROUP:]
    gain_ref, offset_ref, bias_ref, pieces_ref, allowed_ref, *refs = refs
    hidden_ref, normed_ref, packed_ref, weight_ref, out_ref, block_ref = refs
    step = pl.program_id(0)
    width = 2 * HEAD_DIM
    own_rows = weight_ref.shape[0] // pieces_ref.shape[0]

    @pl.when(step == 0)
    def _():
        for part in range(3):
            piece = pieces_ref[:, part * own_rows : (part + 1) * own_rows, :]
            weight_ref[:, part * width : (part + 1) * width] = piece.reshape(-1, width)

    rows = block_ref.shape[0] // 2
    pick_block(step, token_refs[0::2], block_ref.at[pl.ds(0, rows)])
    pick_block(step, token_refs[1::2], block_ref.at[pl.ds(rows, rows)])
    normed, _ = norm_rows(block_ref[...].astype(WIDE))
    hidden = (normed * gain_ref[...] + offset_ref[...]).astype(LOW)
    normed_ref[...] = normed.astype(LOW)
    hidden_ref[...] = hidden
    packed = (plain_dot(hidden, weight_ref[...]) + bias_ref[...]).astype(LOW)
    packed_ref[...] = packed
    odd = (place_ref[0] >> 1) & 1
    for block in range(2):
        part = packed[block * rows : (block + 1) * rows]
        query, key, value = (part[:, k * width : (k + 1) * width] for k in range(3))
        allowed = allowed_ref[odd ^ block, 0] > 0
        total = None
        for mask in head_masks():
            weights = softmax_rows(query * mask, key, allowed).astype(LOW)
            term = plain_dot(weights, value * mask)
            total = term if total is None else total + term
        out_ref[odd ^ block, 0] = total.astype(LOW)


def attention_back_kernel(
    place_ref,
    earlier_ref,
    packed_ref,
    grad_ref,
    allowed_ref,
    weight_ref,
    normed_ref,
    out_ref,
    near_ref,
    far_ref,
    norm_sums_ref,
    bias_sums_ref,
):
    masks = head_masks()
    rows = allowed_ref.shape[2]
    width = 2 * HEAD_DIM
    scale = 1.0 / math.sqrt(HEAD_DIM)
    odd = (place_ref[0] >> 1) & 1
    for block in range(2):
        part = pl.ds(block * rows, rows)
        query = packed_ref[part, :width]
        key = packed_ref[part, width : 2 * width]
        value = packed_ref[part, 2 * width :]
        grad = grad_ref[odd ^ block, 0]
        allowed = allowed_ref[odd ^ block, 0] > 0
        sums = [None, None, None]
        for mask in masks:
            query_head = query * mask
            grad_head = grad * mask
            weights = softmax_rows(query_head, key, allowed)
            grad_weights = right_dot(grad_head, value)
            grad_scores = weights * (
                grad_weights - jnp.sum(grad_weights * weights, axis=1, keepdims=True)
            )
            grad_scores = grad_scores.astype(LOW)
            terms = (
                plain_dot(grad_scores, key * mask),
                left_dot(grad_scores, query_head),
                left_dot(weights.astype(LOW), grad_head),
            )
            sums = [t if s is None else s + t for s, t in zip(sums, terms)]
        out_ref[part, :width] = (sums[0] * scale).astype(LOW)
        out_ref[part, width : 2 * width] = (sums[1] * scale).astype(LOW)
        out_ref[part, 2 * width :] = sums[2].astype(LOW)
    grad_hidden = right_dot(out_ref[...], weight_ref[...])
    hidden = grad_hidden.astype(LOW)
    step = pl.program_id(0)
    gain_sums = jnp.sum(grad_hidden * normed_ref[...].astype(WIDE), axis=0, keepdims=True)
    plain_sums = jnp.sum(grad_hidden, axis=0, keepdims=True)
    norm_sums = jnp.concatenate([gain_sums, plain_sums], axis=0)
    bias_sums = jnp.sum(out_ref[...].astype(WIDE), axis=0, keepdims=True)

    @pl.when(step == 0)
    def _():
        norm_sums_ref[...] = norm_sums
        bias_sums_ref[...] = bias_sums

    @pl.when(step > 0)
    def _():
        norm_sums_ref[...] += norm_sums
        bias_sums_ref[...] += bias_sums

    store_pair(step, odd, hidden, near_ref, far_ref)


def store_pair(step, odd, pair, near_ref, far_ref):
    rows = pair.shape[0] // 2
    first = pl.ds(pl.multiple_of(odd * rows, rows), rows)
    second = pl.ds(pl.multiple_of((1 - odd) * rows, rows), rows)
    half = pl.num_programs(0) // 2
    for ref, wanted in ((near_ref, step < half), (far_ref, step >= half)):

        @pl.when(wanted)
        def _(ref=ref):
            ref[first, :] = pair[:rows]
            ref[second, :] = pair[rows:]


def pair_spec(rows, columns):
    return pl.BlockSpec(
        (2, 1, rows, columns), lambda i, p: ((p[0] >> 2) ^ (i & 1), (p[0] & 1) ^ (i >> 1), 0, 0)
    )


def fixed(shape):
    return pl.BlockSpec(shape, lambda i, p: (0,) * len(shape))


def attention(blocks, gain, offset, bias, pieces, allowed, places):
    rows, model_width = blocks[0].shape
    width = 2 * HEAD_DIM
    count = len(blocks)
    return pl.pallas_call(
        attention_kernel,
        grid_spec=pltpu.PrefetchScalarGridSpec(
            num_scalar_prefetch=1,
            grid=(count // 2,),
            in_specs=[fixed((rows, model_width))] * count
            + [
                fixed((1, model_width)),
                fixed((1, model_width)),
                fixed((1, 3 * width)),
                fixed(pieces.shape),
                pair_spec(rows, rows),
            ],
            out_specs=[
                pl.BlockSpec((2 * rows, model_width), lambda i, p: (i, 0)),
                pl.BlockSpec((2 * rows, model_width), lambda i, p: (i, 0)),
                pl.BlockSpec((2 * rows, 3 * width), lambda i, p: (i, 0)),
                fixed((model_width, 3 * width)),
                pair_spec(rows, width),
            ],
            scratch_shapes=[pltpu.VMEM((2 * rows, model_width), LOW)],
        ),
        out_shape=[
            jax.ShapeDtypeStruct((count * rows, model_width), LOW),
            jax.ShapeDtypeStruct((count * rows, model_width), LOW),
            jax.ShapeDtypeStruct((count * rows, 3 * width), LOW),
            jax.ShapeDtypeStruct((model_width, 3 * width), LOW),
            jax.ShapeDtypeStruct((count // 2, 2, rows, width), LOW),
        ],
        compiler_params=pltpu.CompilerParams(vmem_limit_bytes=VMEM_BYTES),
        cost_estimate=pl.CostEstimate(
            flops=8 * count * rows * rows * width,
            bytes_accessed=count * rows * model_width,
            transcendentals=0,
        ),
    )(places, *blocks, gain, offset, bias, pieces, allowed.reshape(count // 2, 2, rows, rows))


def attention_back(packed, grad, allowed, weight, normed, places, earlier):
    blocks, rows, _ = allowed.shape
    grad = grad.reshape(blocks // 2, 2, rows, -1)
    allowed = allowed.reshape(blocks // 2, 2, rows, rows)
    width = 2 * HEAD_DIM
    model_width = weight.shape[0]
    half = blocks // 2
    return pl.pallas_call(
        attention_back_kernel,
        grid_spec=pltpu.PrefetchScalarGridSpec(
            num_scalar_prefetch=1,
            grid=(blocks // 2,),
            in_specs=[
                pl.BlockSpec(memory_space=pl.ANY),
                pl.BlockSpec((2 * rows, 3 * width), lambda i, p: (i, 0)),
                pair_spec(rows, width),
                pair_spec(rows, rows),
                pl.BlockSpec((model_width, 3 * width), lambda i, p: (0, 0)),
                pl.BlockSpec((2 * rows, model_width), lambda i, p: (i, 0)),
            ],
            out_specs=[
                pl.BlockSpec((2 * rows, 3 * width), lambda i, p: (i, 0)),
                pl.BlockSpec(
                    (2 * rows, model_width), lambda i, p: ((p[0] >> 2) ^ jnp.minimum(i, 1), 0)
                ),
                pl.BlockSpec(
                    (2 * rows, model_width), lambda i, p: ((p[0] >> 2) ^ (jnp.maximum(i, 2) - 2), 0)
                ),
                pl.BlockSpec((2, model_width), lambda i, p: (0, 0)),
                pl.BlockSpec((1, 3 * width), lambda i, p: (0, 0)),
            ],
        ),
        out_shape=[
            jax.ShapeDtypeStruct((blocks * rows, 3 * width), LOW),
            jax.ShapeDtypeStruct((half * rows, model_width), LOW),
            jax.ShapeDtypeStruct((half * rows, model_width), LOW),
            jax.ShapeDtypeStruct((2, model_width), WIDE),
            jax.ShapeDtypeStruct((1, 3 * width), WIDE),
        ],
        compiler_params=pltpu.CompilerParams(vmem_limit_bytes=VMEM_BYTES),
        cost_estimate=pl.CostEstimate(
            flops=20 * blocks * rows * rows * width,
            bytes_accessed=4 * packed.size + 4 * allowed.size,
            transcendentals=2 * allowed.size,
        ),
    )(places, earlier, packed, grad, allowed, weight, normed)


def feed_kernel(place_ref, *refs):
    input_refs, grad_refs, refs = refs[:GROUP], refs[GROUP : 2 * GROUP], refs[2 * GROUP :]
    planes = len(refs) - 11
    up_refs, refs = refs[:planes], refs[planes:]
    down_ref, bias_ref, input_ref, grad_ref, act_ref, pre_ref, sums_ref, near_ref, far_ref = refs[:9]
    up_ref = refs[9]
    step = pl.program_id(0)
    rows = input_ref.shape[0] // 2
    pick_block(step, input_refs[0::2], input_ref.at[pl.ds(0, rows)])
    pick_block(step, input_refs[1::2], input_ref.at[pl.ds(rows, rows)])
    pick_block(step, grad_refs[0::2], grad_ref.at[pl.ds(0, rows)])
    pick_block(step, grad_refs[1::2], grad_ref.at[pl.ds(rows, rows)])

    @pl.when(step == 0)
    def _():
        for k, ref in enumerate(up_refs):
            depth = ref.shape[0] * ref.shape[1]
            source = lax.rem(place_ref[1] + planes - k, planes) * depth
            up_ref[pl.ds(pl.multiple_of(source, depth), depth), :] = ref[...].reshape(depth, -1)

    root, cube = 0.7978845608028654, 0.044715
    pre = plain_dot(input_ref[...], up_ref[...]) + bias_ref[...]
    square = pre * pre
    bend = jnp.tanh(root * (pre + cube * square * pre))
    act_ref[...] = (0.5 * pre * (1.0 + bend)).astype(LOW)
    slope = 0.5 * (1.0 + bend) + 0.5 * pre * (1.0 - bend * bend) * (
        root * (1.0 + 3.0 * cube * square)
    )
    grad_pre = (right_dot(grad_ref[...], down_ref[...]) * slope).astype(LOW)
    pre_ref[...] = grad_pre
    sums = jnp.sum(grad_pre.astype(WIDE), axis=0, keepdims=True)

    @pl.when(step == 0)
    def _():
        sums_ref[...] = sums

    @pl.when(step > 0)
    def _():
        sums_ref[...] += sums

    hidden = right_dot(grad_pre, up_ref[...]).astype(LOW)
    store_pair(step, (place_ref[0] >> 1) & 1, hidden, near_ref, far_ref)


def feed_forward(inputs, grads, up_parts, down, bias, places):
    block_rows, width = inputs[0].shape
    hidden = down.shape[0]
    tokens = GROUP * block_rows
    rows = 2 * block_rows
    steps = tokens // rows
    half = steps // 2
    return pl.pallas_call(
        feed_kernel,
        grid_spec=pltpu.PrefetchScalarGridSpec(
            num_scalar_prefetch=1,
            grid=(steps,),
            in_specs=[fixed((block_rows, width))] * (2 * GROUP)
            + [fixed(part.shape) for part in up_parts]
            + [fixed((hidden, width)), fixed((1, hidden))],
            out_specs=[
                pl.BlockSpec((rows, width), lambda i, p: (i, 0)),
                pl.BlockSpec((rows, width), lambda i, p: (i, 0)),
                pl.BlockSpec((rows, hidden), lambda i, p: (i, 0)),
                pl.BlockSpec((rows, hidden), lambda i, p: (i, 0)),
                fixed((1, hidden)),
                pl.BlockSpec((rows, width), lambda i, p: ((p[0] >> 2) ^ jnp.minimum(i, half - 1), 0)),
                pl.BlockSpec(
                    (rows, width), lambda i, p: ((p[0] >> 2) ^ (jnp.maximum(i, half) - half), 0)
                ),
            ],
            scratch_shapes=[pltpu.VMEM((width, hidden), LOW), pltpu.SMEM((1,), jnp.int32)],
        ),
        out_shape=[
            jax.ShapeDtypeStruct((tokens, width), LOW),
            jax.ShapeDtypeStruct((tokens, width), LOW),
            jax.ShapeDtypeStruct((tokens, hidden), LOW),
            jax.ShapeDtypeStruct((tokens, hidden), LOW),
            jax.ShapeDtypeStruct((1, hidden), WIDE),
            jax.ShapeDtypeStruct((tokens // 2, width), LOW),
            jax.ShapeDtypeStruct((tokens // 2, width), LOW),
        ],
        compiler_params=pltpu.CompilerParams(vmem_limit_bytes=VMEM_BYTES),
        cost_estimate=pl.CostEstimate(
            flops=tokens * width * hidden,
            bytes_accessed=tokens * width,
            transcendentals=0,
        ),
    )(places, *inputs, *grads, *up_parts, down, bias)


def branch_kernel(place_ref, earlier_ref, act_ref, down_ref, out_ref):
    rows = act_ref.shape[0] // 2
    result = plain_dot(act_ref[...], down_ref[...]).astype(LOW)
    odd = (place_ref[0] >> 1) & 1
    out_ref[pl.ds(pl.multiple_of(odd * rows, rows), rows), :] = result[:rows]
    out_ref[pl.ds(pl.multiple_of((1 - odd) * rows, rows), rows), :] = result[rows:]


def branch_terms(act, down, places, earlier):
    tokens, hidden = act.shape
    width = down.shape[1]
    rows = 2 * tokens // GROUP
    return pl.pallas_call(
        branch_kernel,
        grid_spec=pltpu.PrefetchScalarGridSpec(
            num_scalar_prefetch=1,
            grid=(tokens // rows,),
            in_specs=[
                pl.BlockSpec(memory_space=pl.ANY),
                pl.BlockSpec((rows, hidden), lambda i, p: (i, 0)),
                fixed((hidden, width)),
            ],
            out_specs=pl.BlockSpec(
                (rows, width),
                lambda i, p: (2 * ((p[0] & 1) ^ (i >> 1)) + ((p[0] >> 2) ^ (i & 1)), 0),
            ),
        ),
        out_shape=jax.ShapeDtypeStruct((tokens, width), LOW),
        compiler_params=pltpu.CompilerParams(vmem_limit_bytes=VMEM_BYTES),
    )(places, earlier, act, down)


class Links:
    def __init__(self, count):
        self.count = count
        self.planes = count // GROUP
        index = lax.axis_index("dp")
        self.place = index & (GROUP - 1)
        self.plane = index // GROUP

    def swap(self, array, flip):
        return lax.ppermute(array, "dp", [(i, i ^ flip) for i in range(self.count)])

    def shift(self, array, steps):
        hop = steps * GROUP
        return lax.ppermute(array, "dp", [(i, (i + hop) % self.count) for i in range(self.count)])

    def group_gather(self, block):
        near = [block] + [None] * 3
        for k in (3, 1, 2):
            near[k] = self.swap(block, 2 * k)
        far = [self.swap(b, 1) for b in near]
        return near + far

    def core_sum(self, near, far, order=0.0):
        return (near.astype(WIDE) + (self.swap(far, 1).astype(WIDE) + order)).astype(LOW)

    def chip_sum(self, halves):
        total = halves[0].astype(WIDE)
        for k in (3, 1, 2):
            total = total + self.swap(halves[k], 2 * k).astype(WIDE)
        return total

    def chip_exchange(self, halves):
        chips = GROUP // 2
        groups = [
            [p * GROUP + 2 * m + c for m in range(chips)]
            for p in range(self.planes)
            for c in range(2)
        ]
        parts = halves.reshape(chips, halves.shape[0] // chips, halves.shape[1])
        terms = lax.all_to_all(parts, "dp", 0, 0, axis_index_groups=groups, tiled=True)
        return jnp.sum(terms.astype(WIDE), axis=0)

    def core_lists(self):
        order = [2 * m + c for c in range(2) for m in range(GROUP // 2)]
        return [[p * GROUP + j for j in order] for p in range(self.planes)]

    def group_lists(self):
        return [[p * GROUP + j for j in range(GROUP)] for p in range(self.planes)]

    def plane_exchange(self, parts):
        return lax.all_to_all(
            parts, "dp", 0, 0, axis_index_groups=self.plane_groups(), tiled=True
        )

    def exchange(self, parts):
        return lax.all_to_all(
            parts, "dp", 0, 0, axis_index_groups=self.group_lists(), tiled=True
        )

    def plane_groups(self):
        return [[p * GROUP + j for p in range(self.planes)] for j in range(GROUP)]

    def plane_gather(self, block):
        if self.planes > DIRECT_PLANES:
            found = lax.all_gather(block, "dp", axis_index_groups=self.plane_groups())
            return [
                lax.dynamic_index_in_dim(found, (self.plane - k) % self.planes, 0, False)
                for k in range(self.planes)
            ]
        return [block] + [self.shift(block, k) for k in range(1, self.planes)]

    def plane_sum(self, chunks):
        if self.planes > DIRECT_PLANES:
            return lax.psum_scatter(
                chunks.astype(WIDE), "dp", axis_index_groups=self.plane_groups()
            )
        total = lax.dynamic_index_in_dim(chunks, self.plane, 0, False).astype(WIDE)
        for k in range(1, self.planes):
            target = (self.plane + k) % self.planes
            term = lax.dynamic_index_in_dim(chunks, target, 0, False)
            total = total + self.shift(term, k).astype(WIDE)
        return total


def order_zero(array):
    return array[(0,) * array.ndim].astype(WIDE) * 0.0


def local(
    tokens,
    segment_ids,
    pad_mask,
    ln1_gain,
    ln1_bias,
    qkv_weight,
    qkv_bias,
    out_weight,
    out_bias,
    ln2_gain,
    ln2_bias,
    up_weight,
    up_bias,
    down_weight,
    down_bias,
    cotangent,
):
    count = lax.axis_size("dp")
    links = Links(count)
    place, planes = links.place, links.planes
    rows, width = tokens.shape
    own_rows = qkv_weight.shape[0]
    hidden = up_weight.shape[1]
    shard = width // GROUP
    hidden_shard = hidden // GROUP
    own_hidden = hidden // count
    heads_width = 3 * shard

    code = (segment_ids * 2 + pad_mask).astype(LOW)
    fill = jnp.zeros((shard - 4 * own_rows,), LOW)
    wide_fill = jnp.zeros((shard - own_hidden,), LOW)
    empty = jnp.zeros((shard,), LOW)
    small = [
        jnp.concatenate([ln1_gain, ln1_bias, out_bias, ln2_gain, fill]),
        jnp.concatenate([ln2_bias, down_bias, qkv_bias, fill]),
        jnp.concatenate([up_bias, wide_fill]),
        code,
    ]
    small = jnp.stack(small + [empty] * 4)
    qkv_parts = qkv_weight.reshape(own_rows, 3, GROUP, shard).transpose(2, 1, 0, 3)
    qkv_parts = qkv_parts.reshape(GROUP, 3 * own_rows, shard)
    small_parts = jnp.broadcast_to(small[None], (GROUP,) + small.shape)
    sent = jnp.concatenate([qkv_parts, small_parts], axis=1)
    sent = jnp.broadcast_to(sent[None], (planes,) + sent.shape).reshape((count,) + sent.shape[1:])
    up_parts = up_weight.reshape(own_rows, planes, GROUP, own_hidden)
    up_parts = up_parts.transpose(2, 0, 1, 3).reshape(GROUP, own_rows, hidden_shard)
    up_plane = links.exchange(up_parts)
    sent = sent + order_zero(up_plane).astype(LOW)
    token_blocks = links.group_gather(tokens)
    grad_out = cotangent.astype(WIDE) * pad_mask.astype(WIDE)[:, None]
    grad_feed_own = grad_out.astype(LOW)
    grad_feed_blocks = links.group_gather(grad_feed_own)
    buffer = lax.all_to_all(sent, "dp", 0, 0, tiled=True)
    out_full = lax.all_gather(out_weight, "dp", axis=0, tiled=True)
    down_full = lax.all_gather(
        down_weight, "dp", axis_index_groups=links.plane_groups(), tiled=True
    )
    def small_vector(row, start, length):
        start = start * own_rows
        return buffer[:, 3 * own_rows + row, start : start + length].astype(WIDE)

    gain_one, bias_one, bias_out, gain_two, bias_two, bias_down = (
        small_vector(i // 4, i % 4, own_rows).reshape(width) for i in range(6)
    )
    qkv_bias_all = small_vector(1, 2, 2 * own_rows).reshape(2, width)
    bias_qv = lax.dynamic_slice_in_dim(qkv_bias_all, place * shard, shard, 1)
    bias_heads = jnp.concatenate([bias_qv[0], jnp.zeros((shard,), WIDE), bias_qv[1]])
    up_bias_all = small_vector(2, 0, own_hidden).reshape(planes, GROUP, own_hidden)
    bias_up = lax.dynamic_index_in_dim(up_bias_all, place, 1, False).reshape(hidden_shard)

    codes = lax.dynamic_slice_in_dim(small_vector(3, 0, rows), links.plane * GROUP, GROUP, 0)
    codes = codes.astype(jnp.int32)
    segments, live = codes >> 1, codes & 1
    positions = jnp.arange(rows, dtype=jnp.int32)
    allowed = (
        (segments[:, :, None] == segments[:, None, :])
        & (positions[None, :] <= positions[:, None])[None]
        & (live[:, None, :] == 1)
    ).astype(WIDE)

    places = jnp.stack([place, links.plane])
    hidden_one, normed_low, packed, qkv_full, mixed_heads = attention(
        token_blocks,
        gain_one[None],
        bias_one[None],
        bias_heads[None],
        buffer,
        allowed,
        places,
    )
    up_blocks = links.plane_gather(up_plane)
    mixed_heads = mixed_heads.reshape(GROUP, rows, shard)
    mixed = links.exchange(mixed_heads)
    mixed = mixed.transpose(1, 0, 2).reshape(rows, width)
    token_rows = tokens.astype(WIDE)
    middle = token_rows + (plain_dot(mixed, out_full) + bias_out)
    normed_two, inverse_two = norm_rows(middle)
    hidden_two_own = (normed_two * gain_two + bias_two).astype(LOW)
    up_here = sum(order_zero(b) for b in up_blocks[1:])
    hidden_two_own = (hidden_two_own.astype(WIDE) + up_here).astype(LOW)
    hidden_two_blocks = links.group_gather(hidden_two_own)

    half_rows = GROUP * rows // 2
    hidden_two, grad_feed, activated_low, grad_pre_low, up_bias_sums, near, far = feed_forward(
        hidden_two_blocks, grad_feed_blocks, up_blocks, down_full, bias_up[None], places
    )
    grad_hidden_half = links.core_sum(near, far)
    grad_hidden_two = links.chip_exchange(grad_hidden_half)
    grad_middle = grad_out + norm_back(grad_hidden_two, normed_two, inverse_two, gain_two)
    grad_branch = grad_middle.astype(LOW)
    grad_mixed_own = right_dot(grad_branch, out_full).astype(LOW)
    grad_mixed_sent = grad_mixed_own.reshape(rows, GROUP, shard).transpose(1, 0, 2)
    grad_mixed = links.exchange(grad_mixed_sent)
    grad_mixed = grad_mixed.reshape(GROUP * rows, shard)

    out_parts = left_dot(mixed, grad_branch).astype(LOW)
    out_parts = out_parts.reshape(planes, GROUP, own_rows, width)
    out_near, out_far = (
        jnp.stack(
            [lax.dynamic_index_in_dim(out_parts, place ^ r, 1, False) for r in order]
        ).reshape(4, planes * own_rows, width)
        for order in ((0, 2, 4, 6), (1, 3, 5, 7))
    )
    out_half = links.core_sum(out_near, out_far)

    pieces = [left_dot(hidden_two, grad_pre_low).astype(LOW).reshape(planes, -1, hidden_shard)]
    for start in range(0, width, hidden_shard):
        piece = left_dot(activated_low, grad_feed[:, start : start + hidden_shard]).astype(LOW)
        pieces.append(piece.reshape(planes, own_hidden, hidden_shard))
    both_rows = lax.psum_scatter(
        jnp.concatenate(pieces, axis=1), "dp", axis_index_groups=links.plane_groups()
    )
    up_rows = both_rows[: GROUP * own_rows].reshape(GROUP, own_rows, hidden_shard)
    grad_down_w = both_rows[GROUP * own_rows :].reshape(-1, own_hidden, hidden_shard)
    grad_down_w = grad_down_w.transpose(1, 0, 2).reshape(own_hidden, width).astype(WIDE)

    grad_packed, near, far, norm_sums, packed_sums = attention_back(
        packed, grad_mixed, allowed, qkv_full, normed_low, places, out_half
    )
    proj_rows = left_dot(hidden_one, grad_packed).astype(LOW)
    proj_rows = proj_rows.reshape(planes, GROUP, own_rows, heads_width)
    proj_sum = links.plane_sum(proj_rows)
    grad_hidden_half = links.core_sum(near, far)
    grad_hidden_one = links.chip_exchange(grad_hidden_half)
    feed_parts = branch_terms(activated_low, down_full, places, grad_hidden_half)
    feed = lax.psum_scatter(
        feed_parts, "dp", axis_index_groups=links.core_lists(), scatter_dimension=0, tiled=True
    )
    block_out = (middle + feed.astype(WIDE) + bias_down).astype(LOW)
    out_chips = (out_half + order_zero(grad_hidden_one).astype(LOW)).reshape(4, -1, width)
    out_sum = links.chip_sum(out_chips).astype(LOW)
    normed_one, inverse_one = norm_rows(token_rows)
    grad_inputs = grad_middle + norm_back(grad_hidden_one, normed_one, inverse_one, gain_one)

    proj_sums = jnp.zeros((2, width), WIDE)
    proj_sums = lax.dynamic_update_slice_in_dim(
        proj_sums,
        jnp.concatenate([packed_sums[:, :shard], packed_sums[:, 2 * shard :]], axis=0),
        place * shard,
        1,
    )
    up_sums = jnp.zeros((planes, GROUP, own_hidden), WIDE)
    up_sums = lax.dynamic_update_index_in_dim(
        up_sums, up_bias_sums.reshape(planes, own_hidden), place, 1
    )
    vectors = [
        norm_sums[0],
        norm_sums[1],
        jnp.sum(grad_branch.astype(WIDE), axis=0),
        jnp.sum(grad_hidden_two * normed_two, axis=0),
        jnp.sum(grad_hidden_two, axis=0),
        jnp.sum(grad_feed_own.astype(WIDE), axis=0),
        proj_sums,
        up_sums,
    ]
    vectors = jnp.concatenate([v.reshape(planes, GROUP, -1) for v in vectors], axis=2)
    grad_out_w = links.plane_sum(out_sum.reshape(planes, own_rows, width))
    vectors = vectors.reshape(count, -1) + order_zero(grad_hidden_one)
    sums = jnp.sum(lax.all_to_all(vectors, "dp", 0, 0, tiled=True), axis=0)
    proj_rows = (proj_sum + order_zero(sums)).astype(LOW)
    row_blocks = links.exchange(jnp.concatenate([proj_rows, up_rows], axis=2))
    row_blocks = row_blocks.astype(WIDE)
    grad_proj_w = row_blocks[:, :, :heads_width]
    grad_proj_w = grad_proj_w.reshape(GROUP, own_rows, 3, shard).transpose(1, 2, 0, 3)
    grad_proj_w = grad_proj_w.reshape(own_rows, 3 * width)
    grad_up_w = row_blocks[:, :, heads_width:]
    grad_up_w = grad_up_w.reshape(GROUP, own_rows, planes, own_hidden).transpose(1, 2, 0, 3)
    grad_up_w = grad_up_w.reshape(own_rows, hidden)

    grads = [sums[i * own_rows : (i + 1) * own_rows] for i in range(6)]
    grad_proj_b = sums[6 * own_rows : 8 * own_rows]
    grad_up_b = sums[8 * own_rows :]
    return (
        block_out,
        grad_inputs,
        grads[0],
        grads[1],
        grad_proj_w,
        grad_proj_b,
        grad_out_w,
        grads[2],
        grads[3],
        grads[4],
        grad_up_w,
        grad_up_b,
        grad_down_w,
        grads[5],
    )


def solution(mesh):
    flat, wide = P("dp"), P("dp", None)
    in_specs = (
        (wide, flat, flat, flat, flat, wide, flat, wide, flat, flat, flat, wide, flat, wide)
        + (flat, wide)
    )
    out_specs = (
        (wide, wide, flat, flat, wide, flat, wide, flat, flat, flat, wide, flat, wide, flat)
    )
    return jax.shard_map(local, mesh=mesh, in_specs=in_specs, out_specs=out_specs, check_vma=False)
```

```python
import functools
import math

import jax
import jax.numpy as jnp
from jax import lax
from jax.experimental import pallas as pl
from jax.experimental.pallas import tpu as pltpu
from jax.sharding import PartitionSpec as P

HEAD_DIM = 64
EPS = 1e-05
NEG = -1e30
GROUP = 8
DIRECT_PLANES = 8
VMEM_BYTES = 56 << 20
LOW = jnp.bfloat16
WIDE = jnp.float32


def norm_rows(inputs):
    average = jnp.mean(inputs, axis=-1, keepdims=True)
    centered = inputs - average
    variance = jnp.mean(centered * centered, axis=-1, keepdims=True)
    inverse = lax.rsqrt(variance + EPS)
    return (centered * inverse, inverse)


def norm_back(grad_in, normed, inverse, gain):
    scaled = grad_in * gain
    return inverse * (
        scaled
        - jnp.mean(scaled, axis=1, keepdims=True)
        - normed * jnp.mean(scaled * normed, axis=1, keepdims=True)
    )


def gelu_tanh(inputs):
    return (
        0.5
        * inputs
        * (1.0 + jnp.tanh(0.7978845608028654 * (inputs + 0.044715 * inputs * inputs * inputs)))
    )


def dot(first, second, dims):
    return lax.dot_general(first, second, (dims, ((), ())), preferred_element_type=jnp.float32)


def plain_dot(first, second):
    return dot(first, second, ((1,), (0,)))


def left_dot(first, second):
    return dot(first, second, ((0,), (0,)))


def right_dot(first, second):
    return dot(first, second, ((1,), (1,)))


def head_masks():
    lane = lax.broadcasted_iota(jnp.int32, (1, 2 * HEAD_DIM), 1)
    return [((lane // HEAD_DIM) == h).astype(LOW) for h in range(2)]


def softmax_rows(query, key, allowed):
    scores = right_dot(query, key) * (1.0 / math.sqrt(HEAD_DIM))
    scores = jnp.where(allowed, scores, NEG)
    top = jnp.max(scores, axis=1, keepdims=True)
    raw = jnp.exp(scores - top)
    return raw / jnp.sum(raw, axis=1, keepdims=True)


def pick_block(step, refs, target_ref):
    for k, ref in enumerate(refs):

        @pl.when(step == k)
        def _(ref=ref):
            target_ref[...] = ref[...]


def attention_kernel(place_ref, *refs):
    token_refs, refs = refs[:GROUP], refs[GROUP:]
    gain_ref, offset_ref, bias_ref, pieces_ref, allowed_ref, *refs = refs
    hidden_ref, normed_ref, packed_ref, weight_ref, out_ref, block_ref = refs
    step = pl.program_id(0)
    width = 2 * HEAD_DIM
    own_rows = weight_ref.shape[0] // pieces_ref.shape[0]

    @pl.when(step == 0)
    def _():
        for part in range(3):
            piece = pieces_ref[:, part * own_rows : (part + 1) * own_rows, :]
            weight_ref[:, part * width : (part + 1) * width] = piece.reshape(-1, width)

    rows = block_ref.shape[0] // 2
    pick_block(step, token_refs[0::2], block_ref.at[pl.ds(0, rows)])
    pick_block(step, token_refs[1::2], block_ref.at[pl.ds(rows, rows)])
    normed, _ = norm_rows(block_ref[...].astype(WIDE))
    hidden = (normed * gain_ref[...] + offset_ref[...]).astype(LOW)
    normed_ref[...] = normed.astype(LOW)
    hidden_ref[...] = hidden
    packed = (plain_dot(hidden, weight_ref[...]) + bias_ref[...]).astype(LOW)
    packed_ref[...] = packed
    odd = (place_ref[0] >> 1) & 1
    for block in range(2):
        part = packed[block * rows : (block + 1) * rows]
        query, key, value = (part[:, k * width : (k + 1) * width] for k in range(3))
        allowed = allowed_ref[odd ^ block, 0] > 0
        total = None
        for mask in head_masks():
            weights = softmax_rows(query * mask, key, allowed).astype(LOW)
            term = plain_dot(weights, value * mask)
            total = term if total is None else total + term
        out_ref[odd ^ block, 0] = total.astype(LOW)


def attention_back_kernel(
    place_ref,
    earlier_ref,
    packed_ref,
    grad_ref,
    allowed_ref,
    weight_ref,
    normed_ref,
    out_ref,
    near_ref,
    far_ref,
    norm_sums_ref,
    bias_sums_ref,
):
    masks = head_masks()
    rows = allowed_ref.shape[2]
    width = 2 * HEAD_DIM
    scale = 1.0 / math.sqrt(HEAD_DIM)
    odd = (place_ref[0] >> 1) & 1
    for block in range(2):
        part = pl.ds(block * rows, rows)
        query = packed_ref[part, :width]
        key = packed_ref[part, width : 2 * width]
        value = packed_ref[part, 2 * width :]
        grad = grad_ref[odd ^ block, 0]
        allowed = allowed_ref[odd ^ block, 0] > 0
        sums = [None, None, None]
        for mask in masks:
            query_head = query * mask
            grad_head = grad * mask
            weights = softmax_rows(query_head, key, allowed)
            grad_weights = right_dot(grad_head, value)
            grad_scores = weights * (
                grad_weights - jnp.sum(grad_weights * weights, axis=1, keepdims=True)
            )
            grad_scores = grad_scores.astype(LOW)
            terms = (
                plain_dot(grad_scores, key * mask),
                left_dot(grad_scores, query_head),
                left_dot(weights.astype(LOW), grad_head),
            )
            sums = [t if s is None else s + t for s, t in zip(sums, terms)]
        out_ref[part, :width] = (sums[0] * scale).astype(LOW)
        out_ref[part, width : 2 * width] = (sums[1] * scale).astype(LOW)
        out_ref[part, 2 * width :] = sums[2].astype(LOW)
    grad_hidden = right_dot(out_ref[...], weight_ref[...])
    hidden = grad_hidden.astype(LOW)
    step = pl.program_id(0)
    gain_sums = jnp.sum(grad_hidden * normed_ref[...].astype(WIDE), axis=0, keepdims=True)
    plain_sums = jnp.sum(grad_hidden, axis=0, keepdims=True)
    norm_sums = jnp.concatenate([gain_sums, plain_sums], axis=0)
    bias_sums = jnp.sum(out_ref[...].astype(WIDE), axis=0, keepdims=True)

    @pl.when(step == 0)
    def _():
        norm_sums_ref[...] = norm_sums
        bias_sums_ref[...] = bias_sums

    @pl.when(step > 0)
    def _():
        norm_sums_ref[...] += norm_sums
        bias_sums_ref[...] += bias_sums

    store_pair(step, odd, hidden, near_ref, far_ref)


def store_pair(step, odd, pair, near_ref, far_ref):
    rows = pair.shape[0] // 2
    first = pl.ds(pl.multiple_of(odd * rows, rows), rows)
    second = pl.ds(pl.multiple_of((1 - odd) * rows, rows), rows)
    half = pl.num_programs(0) // 2
    for ref, wanted in ((near_ref, step < half), (far_ref, step >= half)):

        @pl.when(wanted)
        def _(ref=ref):
            ref[first, :] = pair[:rows]
            ref[second, :] = pair[rows:]


def pair_spec(rows, columns):
    return pl.BlockSpec(
        (2, 1, rows, columns), lambda i, p: ((p[0] >> 2) ^ (i & 1), (p[0] & 1) ^ (i >> 1), 0, 0)
    )


def fixed(shape):
    return pl.BlockSpec(shape, lambda i, p: (0,) * len(shape))


def attention(blocks, gain, offset, bias, pieces, allowed, places):
    rows, model_width = blocks[0].shape
    width = 2 * HEAD_DIM
    count = len(blocks)
    return pl.pallas_call(
        attention_kernel,
        grid_spec=pltpu.PrefetchScalarGridSpec(
            num_scalar_prefetch=1,
            grid=(count // 2,),
            in_specs=[fixed((rows, model_width))] * count
            + [
                fixed((1, model_width)),
                fixed((1, model_width)),
                fixed((1, 3 * width)),
                fixed(pieces.shape),
                pair_spec(rows, rows),
            ],
            out_specs=[
                pl.BlockSpec((2 * rows, model_width), lambda i, p: (i, 0)),
                pl.BlockSpec((2 * rows, model_width), lambda i, p: (i, 0)),
                pl.BlockSpec((2 * rows, 3 * width), lambda i, p: (i, 0)),
                fixed((model_width, 3 * width)),
                pair_spec(rows, width),
            ],
            scratch_shapes=[pltpu.VMEM((2 * rows, model_width), LOW)],
        ),
        out_shape=[
            jax.ShapeDtypeStruct((count * rows, model_width), LOW),
            jax.ShapeDtypeStruct((count * rows, model_width), LOW),
            jax.ShapeDtypeStruct((count * rows, 3 * width), LOW),
            jax.ShapeDtypeStruct((model_width, 3 * width), LOW),
            jax.ShapeDtypeStruct((count // 2, 2, rows, width), LOW),
        ],
        compiler_params=pltpu.CompilerParams(vmem_limit_bytes=VMEM_BYTES),
        cost_estimate=pl.CostEstimate(
            flops=8 * count * rows * rows * width,
            bytes_accessed=count * rows * model_width,
            transcendentals=0,
        ),
    )(places, *blocks, gain, offset, bias, pieces, allowed.reshape(count // 2, 2, rows, rows))


def attention_back(packed, grad, allowed, weight, normed, places, earlier):
    blocks, rows, _ = allowed.shape
    grad = grad.reshape(blocks // 2, 2, rows, -1)
    allowed = allowed.reshape(blocks // 2, 2, rows, rows)
    width = 2 * HEAD_DIM
    model_width = weight.shape[0]
    half = blocks // 2
    return pl.pallas_call(
        attention_back_kernel,
        grid_spec=pltpu.PrefetchScalarGridSpec(
            num_scalar_prefetch=1,
            grid=(blocks // 2,),
            in_specs=[
                pl.BlockSpec(memory_space=pl.ANY),
                pl.BlockSpec((2 * rows, 3 * width), lambda i, p: (i, 0)),
                pair_spec(rows, width),
                pair_spec(rows, rows),
                pl.BlockSpec((model_width, 3 * width), lambda i, p: (0, 0)),
                pl.BlockSpec((2 * rows, model_width), lambda i, p: (i, 0)),
            ],
            out_specs=[
                pl.BlockSpec((2 * rows, 3 * width), lambda i, p: (i, 0)),
                pl.BlockSpec(
                    (2 * rows, model_width), lambda i, p: ((p[0] >> 2) ^ jnp.minimum(i, 1), 0)
                ),
                pl.BlockSpec(
                    (2 * rows, model_width), lambda i, p: ((p[0] >> 2) ^ (jnp.maximum(i, 2) - 2), 0)
                ),
                pl.BlockSpec((2, model_width), lambda i, p: (0, 0)),
                pl.BlockSpec((1, 3 * width), lambda i, p: (0, 0)),
            ],
        ),
        out_shape=[
            jax.ShapeDtypeStruct((blocks * rows, 3 * width), LOW),
            jax.ShapeDtypeStruct((half * rows, model_width), LOW),
            jax.ShapeDtypeStruct((half * rows, model_width), LOW),
            jax.ShapeDtypeStruct((2, model_width), WIDE),
            jax.ShapeDtypeStruct((1, 3 * width), WIDE),
        ],
        compiler_params=pltpu.CompilerParams(vmem_limit_bytes=VMEM_BYTES),
        cost_estimate=pl.CostEstimate(
            flops=20 * blocks * rows * rows * width,
            bytes_accessed=4 * packed.size + 4 * allowed.size,
            transcendentals=2 * allowed.size,
        ),
    )(places, earlier, packed, grad, allowed, weight, normed)


def feed_kernel(place_ref, *refs):
    input_refs, grad_refs, refs = refs[:GROUP], refs[GROUP : 2 * GROUP], refs[2 * GROUP :]
    planes = len(refs) - 11
    up_refs, refs = refs[:planes], refs[planes:]
    down_ref, bias_ref, input_ref, grad_ref, act_ref, pre_ref, sums_ref, near_ref, far_ref = refs[:9]
    up_ref = refs[9]
    step = pl.program_id(0)
    rows = input_ref.shape[0] // 2
    pick_block(step, input_refs[0::2], input_ref.at[pl.ds(0, rows)])
    pick_block(step, input_refs[1::2], input_ref.at[pl.ds(rows, rows)])
    pick_block(step, grad_refs[0::2], grad_ref.at[pl.ds(0, rows)])
    pick_block(step, grad_refs[1::2], grad_ref.at[pl.ds(rows, rows)])

    @pl.when(step == 0)
    def _():
        for k, ref in enumerate(up_refs):
            depth = ref.shape[0] * ref.shape[1]
            source = lax.rem(place_ref[1] + planes - k, planes) * depth
            up_ref[pl.ds(pl.multiple_of(source, depth), depth), :] = ref[...].reshape(depth, -1)

    root, cube = 0.7978845608028654, 0.044715
    pre = plain_dot(input_ref[...], up_ref[...]) + bias_ref[...]
    square = pre * pre
    bend = jnp.tanh(root * (pre + cube * square * pre))
    act_ref[...] = (0.5 * pre * (1.0 + bend)).astype(LOW)
    slope = 0.5 * (1.0 + bend) + 0.5 * pre * (1.0 - bend * bend) * (
        root * (1.0 + 3.0 * cube * square)
    )
    grad_pre = (right_dot(grad_ref[...], down_ref[...]) * slope).astype(LOW)
    pre_ref[...] = grad_pre
    sums = jnp.sum(grad_pre.astype(WIDE), axis=0, keepdims=True)

    @pl.when(step == 0)
    def _():
        sums_ref[...] = sums

    @pl.when(step > 0)
    def _():
        sums_ref[...] += sums

    hidden = right_dot(grad_pre, up_ref[...]).astype(LOW)
    store_pair(step, (place_ref[0] >> 1) & 1, hidden, near_ref, far_ref)


def feed_forward(inputs, grads, up_parts, down, bias, places):
    block_rows, width = inputs[0].shape
    hidden = down.shape[0]
    tokens = GROUP * block_rows
    rows = 2 * block_rows
    steps = tokens // rows
    half = steps // 2
    return pl.pallas_call(
        feed_kernel,
        grid_spec=pltpu.PrefetchScalarGridSpec(
            num_scalar_prefetch=1,
            grid=(steps,),
            in_specs=[fixed((block_rows, width))] * (2 * GROUP)
            + [fixed(part.shape) for part in up_parts]
            + [fixed((hidden, width)), fixed((1, hidden))],
            out_specs=[
                pl.BlockSpec((rows, width), lambda i, p: (i, 0)),
                pl.BlockSpec((rows, width), lambda i, p: (i, 0)),
                pl.BlockSpec((rows, hidden), lambda i, p: (i, 0)),
                pl.BlockSpec((rows, hidden), lambda i, p: (i, 0)),
                fixed((1, hidden)),
                pl.BlockSpec((rows, width), lambda i, p: ((p[0] >> 2) ^ jnp.minimum(i, half - 1), 0)),
                pl.BlockSpec(
                    (rows, width), lambda i, p: ((p[0] >> 2) ^ (jnp.maximum(i, half) - half), 0)
                ),
            ],
            scratch_shapes=[pltpu.VMEM((width, hidden), LOW), pltpu.SMEM((1,), jnp.int32)],
        ),
        out_shape=[
            jax.ShapeDtypeStruct((tokens, width), LOW),
            jax.ShapeDtypeStruct((tokens, width), LOW),
            jax.ShapeDtypeStruct((tokens, hidden), LOW),
            jax.ShapeDtypeStruct((tokens, hidden), LOW),
            jax.ShapeDtypeStruct((1, hidden), WIDE),
            jax.ShapeDtypeStruct((tokens // 2, width), LOW),
            jax.ShapeDtypeStruct((tokens // 2, width), LOW),
        ],
        compiler_params=pltpu.CompilerParams(vmem_limit_bytes=VMEM_BYTES),
        cost_estimate=pl.CostEstimate(
            flops=tokens * width * hidden,
            bytes_accessed=tokens * width,
            transcendentals=0,
        ),
    )(places, *inputs, *grads, *up_parts, down, bias)


def branch_kernel(place_ref, earlier_ref, act_ref, down_ref, out_ref):
    rows = act_ref.shape[0] // 2
    result = plain_dot(act_ref[...], down_ref[...]).astype(LOW)
    odd = (place_ref[0] >> 1) & 1
    out_ref[pl.ds(pl.multiple_of(odd * rows, rows), rows), :] = result[:rows]
    out_ref[pl.ds(pl.multiple_of((1 - odd) * rows, rows), rows), :] = result[rows:]


def branch_terms(act, down, places, earlier):
    tokens, hidden = act.shape
    width = down.shape[1]
    rows = 2 * tokens // GROUP
    return pl.pallas_call(
        branch_kernel,
        grid_spec=pltpu.PrefetchScalarGridSpec(
            num_scalar_prefetch=1,
            grid=(tokens // rows,),
            in_specs=[
                pl.BlockSpec(memory_space=pl.ANY),
                pl.BlockSpec((rows, hidden), lambda i, p: (i, 0)),
                fixed((hidden, width)),
            ],
            out_specs=pl.BlockSpec(
                (rows, width),
                lambda i, p: (2 * ((p[0] & 1) ^ (i >> 1)) + ((p[0] >> 2) ^ (i & 1)), 0),
            ),
        ),
        out_shape=jax.ShapeDtypeStruct((tokens, width), LOW),
        compiler_params=pltpu.CompilerParams(vmem_limit_bytes=VMEM_BYTES),
    )(places, earlier, act, down)


class Links:
    def __init__(self, count):
        self.count = count
        self.planes = count // GROUP
        index = lax.axis_index("dp")
        self.place = index & (GROUP - 1)
        self.plane = index // GROUP

    def swap(self, array, flip):
        return lax.ppermute(array, "dp", [(i, i ^ flip) for i in range(self.count)])

    def shift(self, array, steps):
        hop = steps * GROUP
        return lax.ppermute(array, "dp", [(i, (i + hop) % self.count) for i in range(self.count)])

    def group_gather(self, block):
        near = [block] + [None] * 3
        for k in (3, 1, 2):
            near[k] = self.swap(block, 2 * k)
        far = [self.swap(b, 1) for b in near]
        return near + far

    def core_sum(self, near, far, order=0.0):
        return (near.astype(WIDE) + (self.swap(far, 1).astype(WIDE) + order)).astype(LOW)

    def chip_sum(self, halves):
        total = halves[0].astype(WIDE)
        for k in (3, 1, 2):
            total = total + self.swap(halves[k], 2 * k).astype(WIDE)
        return total

    def chip_exchange(self, halves):
        chips = GROUP // 2
        groups = [
            [p * GROUP + 2 * m + c for m in range(chips)]
            for p in range(self.planes)
            for c in range(2)
        ]
        parts = halves.reshape(chips, halves.shape[0] // chips, halves.shape[1])
        terms = lax.all_to_all(parts, "dp", 0, 0, axis_index_groups=groups, tiled=True)
        return jnp.sum(terms.astype(WIDE), axis=0)

    def core_lists(self):
        order = [2 * m + c for c in range(2) for m in range(GROUP // 2)]
        return [[p * GROUP + j for j in order] for p in range(self.planes)]

    def group_lists(self):
        return [[p * GROUP + j for j in range(GROUP)] for p in range(self.planes)]

    def plane_exchange(self, parts):
        return lax.all_to_all(
            parts, "dp", 0, 0, axis_index_groups=self.plane_groups(), tiled=True
        )

    def exchange(self, parts):
        return lax.all_to_all(
            parts, "dp", 0, 0, axis_index_groups=self.group_lists(), tiled=True
        )

    def plane_groups(self):
        return [[p * GROUP + j for p in range(self.planes)] for j in range(GROUP)]

    def plane_gather(self, block):
        if self.planes > DIRECT_PLANES:
            found = lax.all_gather(block, "dp", axis_index_groups=self.plane_groups())
            return [
                lax.dynamic_index_in_dim(found, (self.plane - k) % self.planes, 0, False)
                for k in range(self.planes)
            ]
        return [block] + [self.shift(block, k) for k in range(1, self.planes)]

    def plane_sum(self, chunks):
        if self.planes > DIRECT_PLANES:
            return lax.psum_scatter(
                chunks.astype(WIDE), "dp", axis_index_groups=self.plane_groups()
            )
        total = lax.dynamic_index_in_dim(chunks, self.plane, 0, False).astype(WIDE)
        for k in range(1, self.planes):
            target = (self.plane + k) % self.planes
            term = lax.dynamic_index_in_dim(chunks, target, 0, False)
            total = total + self.shift(term, k).astype(WIDE)
        return total


def order_zero(array):
    return array[(0,) * array.ndim].astype(WIDE) * 0.0


def local(
    tokens,
    segment_ids,
    pad_mask,
    ln1_gain,
    ln1_bias,
    qkv_weight,
    qkv_bias,
    out_weight,
    out_bias,
    ln2_gain,
    ln2_bias,
    up_weight,
    up_bias,
    down_weight,
    down_bias,
    cotangent,
):
    count = lax.axis_size("dp")
    links = Links(count)
    place, planes = links.place, links.planes
    rows, width = tokens.shape
    own_rows = qkv_weight.shape[0]
    hidden = up_weight.shape[1]
    shard = width // GROUP
    hidden_shard = hidden // GROUP
    own_hidden = hidden // count
    heads_width = 3 * shard

    code = (segment_ids * 2 + pad_mask).astype(LOW)
    fill = jnp.zeros((shard - 4 * own_rows,), LOW)
    wide_fill = jnp.zeros((shard - own_hidden,), LOW)
    empty = jnp.zeros((shard,), LOW)
    small = [
        jnp.concatenate([ln1_gain, ln1_bias, out_bias, ln2_gain, fill]),
        jnp.concatenate([ln2_bias, down_bias, qkv_bias, fill]),
        jnp.concatenate([up_bias, wide_fill]),
        code,
    ]
    small = jnp.stack(small + [empty] * 4)
    qkv_parts = qkv_weight.reshape(own_rows, 3, GROUP, shard).transpose(2, 1, 0, 3)
    qkv_parts = qkv_parts.reshape(GROUP, 3 * own_rows, shard)
    small_parts = jnp.broadcast_to(small[None], (GROUP,) + small.shape)
    sent = jnp.concatenate([qkv_parts, small_parts], axis=1)
    sent = jnp.broadcast_to(sent[None], (planes,) + sent.shape).reshape((count,) + sent.shape[1:])
    up_parts = up_weight.reshape(own_rows, planes, GROUP, own_hidden)
    up_parts = up_parts.transpose(2, 0, 1, 3).reshape(GROUP, own_rows, hidden_shard)
    up_plane = links.exchange(up_parts)
    sent = sent + order_zero(up_plane).astype(LOW)
    token_blocks = links.group_gather(tokens)
    grad_out = cotangent.astype(WIDE) * pad_mask.astype(WIDE)[:, None]
    grad_feed_own = grad_out.astype(LOW)
    grad_feed_blocks = links.group_gather(grad_feed_own)
    buffer = lax.all_to_all(sent, "dp", 0, 0, tiled=True)
    out_full = lax.all_gather(out_weight, "dp", axis=0, tiled=True)
    down_full = lax.all_gather(
        down_weight, "dp", axis_index_groups=links.plane_groups(), tiled=True
    )
    def small_vector(row, start, length):
        start = start * own_rows
        return buffer[:, 3 * own_rows + row, start : start + length].astype(WIDE)

    gain_one, bias_one, bias_out, gain_two, bias_two, bias_down = (
        small_vector(i // 4, i % 4, own_rows).reshape(width) for i in range(6)
    )
    qkv_bias_all = small_vector(1, 2, 2 * own_rows).reshape(2, width)
    bias_qv = lax.dynamic_slice_in_dim(qkv_bias_all, place * shard, shard, 1)
    bias_heads = jnp.concatenate([bias_qv[0], jnp.zeros((shard,), WIDE), bias_qv[1]])
    up_bias_all = small_vector(2, 0, own_hidden).reshape(planes, GROUP, own_hidden)
    bias_up = lax.dynamic_index_in_dim(up_bias_all, place, 1, False).reshape(hidden_shard)

    codes = lax.dynamic_slice_in_dim(small_vector(3, 0, rows), links.plane * GROUP, GROUP, 0)
    codes = codes.astype(jnp.int32)
    segments, live = codes >> 1, codes & 1
    positions = jnp.arange(rows, dtype=jnp.int32)
    allowed = (
        (segments[:, :, None] == segments[:, None, :])
        & (positions[None, :] <= positions[:, None])[None]
        & (live[:, None, :] == 1)
    ).astype(WIDE)

    places = jnp.stack([place, links.plane])
    hidden_one, normed_low, packed, qkv_full, mixed_heads = attention(
        token_blocks,
        gain_one[None],
        bias_one[None],
        bias_heads[None],
        buffer,
        allowed,
        places,
    )
    up_blocks = links.plane_gather(up_plane)
    mixed_heads = mixed_heads.reshape(GROUP, rows, shard)
    mixed = links.exchange(mixed_heads)
    mixed = mixed.transpose(1, 0, 2).reshape(rows, width)
    token_rows = tokens.astype(WIDE)
    middle = token_rows + (plain_dot(mixed, out_full) + bias_out)
    normed_two, inverse_two = norm_rows(middle)
    hidden_two_own = (normed_two * gain_two + bias_two).astype(LOW)
    up_here = sum(order_zero(b) for b in up_blocks[1:])
    hidden_two_own = (hidden_two_own.astype(WIDE) + up_here).astype(LOW)
    hidden_two_blocks = links.group_gather(hidden_two_own)

    half_rows = GROUP * rows // 2
    hidden_two, grad_feed, activated_low, grad_pre_low, up_bias_sums, near, far = feed_forward(
        hidden_two_blocks, grad_feed_blocks, up_blocks, down_full, bias_up[None], places
    )
    grad_hidden_half = links.core_sum(near, far)
    grad_hidden_two = links.chip_exchange(grad_hidden_half)
    grad_middle = grad_out + norm_back(grad_hidden_two, normed_two, inverse_two, gain_two)
    grad_branch = grad_middle.astype(LOW)
    grad_mixed_own = right_dot(grad_branch, out_full).astype(LOW)
    grad_mixed_sent = grad_mixed_own.reshape(rows, GROUP, shard).transpose(1, 0, 2)
    grad_mixed = links.exchange(grad_mixed_sent)
    grad_mixed = grad_mixed.reshape(GROUP * rows, shard)

    out_parts = left_dot(mixed, grad_branch).astype(LOW)
    out_parts = out_parts.reshape(planes, GROUP, own_rows, width)
    out_near, out_far = (
        jnp.stack(
            [lax.dynamic_index_in_dim(out_parts, place ^ r, 1, False) for r in order]
        ).reshape(4, planes * own_rows, width)
        for order in ((0, 2, 4, 6), (1, 3, 5, 7))
    )
    out_half = links.core_sum(out_near, out_far)

    pieces = [left_dot(hidden_two, grad_pre_low).astype(LOW).reshape(planes, -1, hidden_shard)]
    for start in range(0, width, hidden_shard):
        piece = left_dot(activated_low, grad_feed[:, start : start + hidden_shard]).astype(LOW)
        pieces.append(piece.reshape(planes, own_hidden, hidden_shard))
    both_rows = lax.psum_scatter(
        jnp.concatenate(pieces, axis=1), "dp", axis_index_groups=links.plane_groups()
    )
    up_rows = both_rows[: GROUP * own_rows].reshape(GROUP, own_rows, hidden_shard)
    grad_down_w = both_rows[GROUP * own_rows :].reshape(-1, own_hidden, hidden_shard)
    grad_down_w = grad_down_w.transpose(1, 0, 2).reshape(own_hidden, width).astype(WIDE)

    grad_packed, near, far, norm_sums, packed_sums = attention_back(
        packed, grad_mixed, allowed, qkv_full, normed_low, places, out_half
    )
    grad_hidden_half = links.core_sum(near, far)
    feed_parts = branch_terms(activated_low, down_full, places, grad_hidden_half)
    proj_rows = (left_dot(hidden_one, grad_packed) + order_zero(feed_parts)).astype(LOW)
    proj_rows = proj_rows.reshape(planes, GROUP, own_rows, heads_width)
    proj_sum = links.plane_sum(proj_rows)
    grad_hidden_one = links.chip_exchange(grad_hidden_half)
    feed = lax.psum_scatter(
        feed_parts, "dp", axis_index_groups=links.core_lists(), scatter_dimension=0, tiled=True
    )
    block_out = (middle + feed.astype(WIDE) + bias_down).astype(LOW)
    out_chips = (out_half + order_zero(grad_hidden_one).astype(LOW)).reshape(4, -1, width)
    out_sum = links.chip_sum(out_chips).astype(LOW)
    normed_one, inverse_one = norm_rows(token_rows)
    grad_inputs = grad_middle + norm_back(grad_hidden_one, normed_one, inverse_one, gain_one)

    proj_sums = jnp.zeros((2, width), WIDE)
    proj_sums = lax.dynamic_update_slice_in_dim(
        proj_sums,
        jnp.concatenate([packed_sums[:, :shard], packed_sums[:, 2 * shard :]], axis=0),
        place * shard,
        1,
    )
    up_sums = jnp.zeros((planes, GROUP, own_hidden), WIDE)
    up_sums = lax.dynamic_update_index_in_dim(
        up_sums, up_bias_sums.reshape(planes, own_hidden), place, 1
    )
    vectors = [
        norm_sums[0],
        norm_sums[1],
        jnp.sum(grad_branch.astype(WIDE), axis=0),
        jnp.sum(grad_hidden_two * normed_two, axis=0),
        jnp.sum(grad_hidden_two, axis=0),
        jnp.sum(grad_feed_own.astype(WIDE), axis=0),
        proj_sums,
        up_sums,
    ]
    vectors = jnp.concatenate([v.reshape(planes, GROUP, -1) for v in vectors], axis=2)
    grad_out_w = links.plane_sum(out_sum.reshape(planes, own_rows, width))
    vectors = vectors.reshape(count, -1) + order_zero(out_chips)
    sums = jnp.sum(lax.all_to_all(vectors, "dp", 0, 0, tiled=True), axis=0)
    proj_rows = (proj_sum + order_zero(sums)).astype(LOW)
    row_blocks = links.exchange(jnp.concatenate([proj_rows, up_rows], axis=2))
    row_blocks = row_blocks.astype(WIDE)
    grad_proj_w = row_blocks[:, :, :heads_width]
    grad_proj_w = grad_proj_w.reshape(GROUP, own_rows, 3, shard).transpose(1, 2, 0, 3)
    grad_proj_w = grad_proj_w.reshape(own_rows, 3 * width)
    grad_up_w = row_blocks[:, :, heads_width:]
    grad_up_w = grad_up_w.reshape(GROUP, own_rows, planes, own_hidden).transpose(1, 2, 0, 3)
    grad_up_w = grad_up_w.reshape(own_rows, hidden)

    grads = [sums[i * own_rows : (i + 1) * own_rows] for i in range(6)]
    grad_proj_b = sums[6 * own_rows : 8 * own_rows]
    grad_up_b = sums[8 * own_rows :]
    return (
        block_out,
        grad_inputs,
        grads[0],
        grads[1],
        grad_proj_w,
        grad_proj_b,
        grad_out_w,
        grads[2],
        grads[3],
        grads[4],
        grad_up_w,
        grad_up_b,
        grad_down_w,
        grads[5],
    )


def solution(mesh):
    flat, wide = P("dp"), P("dp", None)
    in_specs = (
        (wide, flat, flat, flat, flat, wide, flat, wide, flat, flat, flat, wide, flat, wide)
        + (flat, wide)
    )
    out_specs = (
        (wide, wide, flat, flat, wide, flat, wide, flat, flat, flat, wide, flat, wide, flat)
    )
    return jax.shard_map(local, mesh=mesh, in_specs=in_specs, out_specs=out_specs, check_vma=False)
```
